32 devices in a mesh: uly: 4 (over x, core), blk: 8 (over z, y).
Axes of the slice: x: 2, y: 2, z: 4, core: 2. Of those that a mesh axis runs over, the one named last changes fastest.
Arguments:
- tokens: bfloat16 [8, 512, 3072], P('blk', 'uly'), may hold values from -18 to 18
- query_weight: bfloat16 [3072, 32, 128], P('blk', 'uly'), may hold values from -0.109375 to 0.109375
- key_values: bfloat16 [8, 512, 32, 256], P('blk', 'uly'), may hold values from -18 to 18
Outputs:
- attended: bfloat16 [8, 512, 32, 128], P('blk', 'uly')
The draws below stay inside these ranges and needn't reach their ends.
All inputs are finite; a program needn't handle non-finite values.
Results may differ from the reference program's by a relative error of at most 0.012.
Values may be sent and summed in bfloat16 or wider, within the bound.
A program may use at most 64 MiB of HBM per device.

```python
import jax
import jax.numpy as jnp
from jax import lax

D = 3072
H = 32
DH = 128
SEQ = 512
BATCH = 8


def spread_rows(key, shape):
    first = jax.random.fold_in(key, 0)
    return jnp.clip(jax.random.normal(first, shape, jnp.float32), -6.0, 6.0)


def draw_tokens(key, part):
    key = jax.random.fold_in(key, 11)
    return spread_rows(key, (BATCH, SEQ, D)).astype(jnp.bfloat16)


def draw_key_values(key, part):
    key = jax.random.fold_in(key, 23)
    return spread_rows(key, (BATCH, SEQ, H, 2 * DH)).astype(jnp.bfloat16)


def shard_levels(stream_key, shape, cuts, least, top_value):
    level, own = 1.0, jax.random.fold_in(stream_key, 6)
    for position, shards_of in cuts:
        heights = jnp.exp(jax.random.uniform(jax.random.fold_in(own, position), (shards_of,), jnp.float32, least / len(cuts), top_value / len(cuts)))
        level = level * jnp.repeat(heights, shape[position] // shards_of).reshape([-1 if axis == position else 1 for axis in range(len(shape))])
    return level


def normal_values(stream_key, extent, deviation, most, shards=(), dtype=jnp.bfloat16):
    result = jax.random.normal(stream_key, extent, jnp.float32) * deviation
    if len(shards) > 0:
        result = shard_levels(stream_key, extent, shards, -0.22, 0.18) * result
    return jnp.clip(result, min=-most, max=most).astype(dtype)


def setup_inputs(seed: int = 0) -> dict:
    seeds = jax.random.split(jax.random.key(seed), 4)
    tokens = draw_tokens(jax.random.fold_in(seeds[3], 71), 0)
    query_weight = normal_values(seeds[1], (D, H, DH), D ** -0.5, 0.109375, ((0, 8), (1, 4)))
    key_values = draw_key_values(jax.random.fold_in(seeds[3], 71), 0)
    return {"tokens": tokens, "query_weight": query_weight, "key_values": key_values}


def one_sequence(sequence_tokens, sequence_kv, query_weight):
    flat_weight = query_weight.reshape(D, H * DH)
    projected = jnp.dot(sequence_tokens, flat_weight, preferred_element_type=jnp.float32).astype(jnp.bfloat16)
    queries = jnp.transpose(projected.reshape(SEQ, H, DH), (1, 0, 2))
    key_rows = jnp.transpose(sequence_kv[:, :, :DH], (1, 0, 2))
    value_rows = jnp.transpose(sequence_kv[:, :, DH:], (1, 0, 2))
    score_scale = DH ** -0.5

    def one_head(operands):
        query_h, key_h, value_h = operands
        scores = jnp.dot(query_h, key_h.T, preferred_element_type=jnp.float32) * score_scale
        row_max = jnp.max(scores, axis=1, keepdims=True)
        soft = jnp.exp(scores - row_max)
        row_sum = jnp.sum(soft, axis=1, keepdims=True)
        weighted = jnp.dot(soft.astype(jnp.bfloat16), value_h, preferred_element_type=jnp.float32)
        return (weighted / row_sum).astype(jnp.bfloat16)

    stacked = lax.map(one_head, (queries, key_rows, value_rows))
    return jnp.transpose(stacked, (1, 0, 2))


def reference(tokens, query_weight, key_values):
    return lax.map(lambda pair: one_sequence(pair[0], pair[1], query_weight), (tokens, key_values))
```

```python
import functools

import jax
import jax.numpy as jnp
from jax import lax
from jax.experimental import pallas as pl
from jax.experimental.pallas import tpu as pltpu
from jax.sharding import PartitionSpec as P

MESH = pl.DeviceIdType.MESH
CHUNK_HEADS = 2
QUERY_ROWS = 256


def kernel(
    n,
    blocks,
    head_width,
    chunks,
    tok_in,
    w_in,
    kv_in,
    out_ref,
    tok,
    wbuf,
    kvbuf,
    att,
    qbuf,
    loc_sem,
    tok_send,
    tok_fwd,
    tok_recv,
    w_send,
    w_recv,
    kv_send,
    kv_recv,
    out_send,
    out_recv,
    out_loc,
):
    u = lax.axis_index("uly")
    b = lax.axis_index("blk")
    line = blocks // 2
    z = b // 2
    y = b % 2
    mate = z * 2 + (1 - y)
    core_mate = u + 1 - 2 * (u % 2)
    seq_rows = tok_in.shape[0]
    shard = w_in.shape[0]
    width = w_in.shape[1]
    cols = width // chunks
    kv_width = 2 * width
    kv_cols = 2 * cols
    total_rows = n * seq_rows

    def ds(start, size):
        return pl.ds(pl.multiple_of(start * size, size), size)

    def remote(src, dst, send, recv, device):
        return pltpu.make_async_remote_copy(
            src_ref=src, dst_ref=dst, send_sem=send, recv_sem=recv,
            device_id=device, device_id_type=MESH,
        )

    has_up = z < line - 1
    has_down = z > 0

    barrier = pltpu.get_barrier_semaphore()

    def greet(device):
        pl.semaphore_signal(barrier, inc=1, device_id=device, device_id_type=MESH)

    for k in range(1, n):
        greet({"uly": (u + k) % n})
    greet({"blk": mate})

    @pl.when(has_up)
    def _():
        greet({"blk": b + 2})

    @pl.when(has_down)
    def _():
        greet({"blk": b - 2})

    inner = jnp.logical_and(has_up, has_down)

    @pl.when(inner)
    def _():
        pl.semaphore_wait(barrier, n + 2)

    @pl.when(jnp.logical_and(jnp.logical_not(inner), jnp.logical_or(has_up, has_down)))
    def _():
        pl.semaphore_wait(barrier, n + 1)

    @pl.when(jnp.logical_not(jnp.logical_or(has_up, has_down)))
    def _():
        pl.semaphore_wait(barrier, n)

    def piece(c, s):
        return wbuf.at[ds(s, shard), ds(c, cols)]

    UP, DOWN, ACROSS = 0, 1, 2

    def w_copy(c, s, way, own=False):
        step = (2, -2, 0)[way]
        device = mate if way == ACROSS else b + step
        src = w_in.at[:, ds(c, cols)] if own else piece(c, s)
        return remote(src, piece(c, s), w_send.at[way, c, s], w_recv.at[c, s], {"blk": device})

    def own_weights(c):
        w_copy(c, b, ACROSS, True).start()

        @pl.when(has_up)
        def _():
            w_copy(c, b, UP, True).start()

        @pl.when(has_down)
        def _():
            w_copy(c, b, DOWN, True).start()

    def pass_on(c):
        for d in range(1, line):
            @pl.when(z - d >= 0)
            def _():
                s = b - 2 * d
                w_copy(c, s, ACROSS).wait_recv()

                @pl.when(has_up)
                def _():
                    w_copy(c, s, UP).start()

                w_copy(c, s, ACROSS).start()

            @pl.when(z + d < line)
            def _():
                s = b + 2 * d
                w_copy(c, s, ACROSS).wait_recv()

                @pl.when(has_down)
                def _():
                    w_copy(c, s, DOWN).start()

                w_copy(c, s, ACROSS).start()

    def across_arrived(c):
        for j in range(line):
            w_copy(c, 2 * j + 1 - y, ACROSS).wait_recv()

    def weights_sent(c):
        for j in range(line):
            s = 2 * j + y
            w_copy(c, s, ACROSS).wait_send()

            @pl.when(jnp.logical_and(has_up, j <= z))
            def _():
                w_copy(c, s, UP).wait_send()

            @pl.when(jnp.logical_and(has_down, j >= z))
            def _():
                w_copy(c, s, DOWN).wait_send()

    def token_rows(s):
        return tok.at[ds(s, seq_rows), :]

    def token_copy(k):
        return remote(tok_in, token_rows(u), tok_send.at[k], tok_recv.at[u], {"uly": (u + k) % n})

    def token_mate():
        return remote(tok_in, token_rows(u), tok_send.at[1], tok_recv.at[u], {"uly": core_mate})

    def token_forward(k):
        s = (u + n - k) % n
        return remote(token_rows(s), token_rows(s), tok_fwd.at[k], tok_recv.at[s], {"uly": core_mate})

    def token_arrival(s):
        return remote(token_rows(s), token_rows(s), tok_fwd.at[0], tok_recv.at[s], {"uly": core_mate})

    def kv_copy(c, k):
        to = (u + k) % n
        src = kv_in.at[:, pl.ds(pl.multiple_of(to * kv_width + c * kv_cols, kv_cols), kv_cols)]
        dst = kvbuf.at[ds(u, seq_rows), ds(c, kv_cols)]
        return remote(src, dst, kv_send.at[c, k], kv_recv.at[c, u], {"uly": to})

    def kv_arrival(c, k):
        s = (u + n - k) % n
        dst = kvbuf.at[ds(s, seq_rows), ds(c, kv_cols)]
        return remote(dst, dst, kv_send.at[c, k], kv_recv.at[c, s], {"uly": s})

    def out_place(s, c):
        return out_ref.at[:, pl.ds(pl.multiple_of(s * width + c * cols, cols), cols)]

    def out_copy(c, k):
        to = (u + k) % n
        src = att.at[ds(to, seq_rows), ds(c, cols)]
        return remote(src, out_place(u, c), out_send.at[c, k], out_recv.at[c, u], {"uly": to})

    def out_arrival(c, k):
        s = (u + n - k) % n
        src = att.at[ds(s, seq_rows), ds(c, cols)]
        return remote(src, out_place(s, c), out_send.at[c, k], out_recv.at[c, s], {"uly": s})

    def out_own(c):
        return pltpu.make_async_copy(att.at[ds(u, seq_rows), ds(c, cols)], out_place(u, c), out_loc.at[c])

    own_weights(0)
    for k in range(2, n, 2):
        token_copy(k).start()
    token_mate().start()
    for k in range(1, n):
        kv_copy(0, k).start()
    locals_ = (
        pltpu.make_async_copy(w_in, wbuf.at[ds(b, shard), :], loc_sem.at[0]),
        pltpu.make_async_copy(tok_in, token_rows(u), loc_sem.at[1]),
        pltpu.make_async_copy(
            kv_in.at[:, ds(u, kv_width)], kvbuf.at[ds(u, seq_rows), :], loc_sem.at[2]
        ),
    )
    for copy in locals_:
        copy.start()
    for copy in locals_:
        copy.wait()

    scale = head_width ** (-0.5)
    block = min(QUERY_ROWS, total_rows)

    def attend(c):
        def rows_step(r, carry):
            rows = pl.ds(pl.multiple_of(r * block, block), block)
            qbuf[rows, :] = jnp.dot(
                tok[rows, :], wbuf[:, ds(c, cols)], preferred_element_type=jnp.float32
            ).astype(jnp.bfloat16)
            for h in range(cols // head_width):
                q = qbuf[rows, h * head_width:(h + 1) * head_width]
                at = c * kv_cols + 2 * h * head_width
                k = kvbuf[:, pl.ds(pl.multiple_of(at, head_width), head_width)]
                v = kvbuf[:, pl.ds(pl.multiple_of(at + head_width, head_width), head_width)]
                scores = lax.dot_general(
                    q, k, (((1,), (1,)), ((), ())), preferred_element_type=jnp.float32
                ) * scale
                soft = jnp.exp(scores - jnp.max(scores, axis=1, keepdims=True))
                row_sum = jnp.sum(soft, axis=1, keepdims=True)
                weighted = jnp.dot(
                    soft.astype(jnp.bfloat16), v, preferred_element_type=jnp.float32
                )
                place = pl.ds(pl.multiple_of(c * cols + h * head_width, head_width), head_width)
                att[rows, place] = (weighted / row_sum).astype(jnp.bfloat16)
            return carry

        lax.fori_loop(0, total_rows // block, rows_step, 0)

    def chunk_step(i, carry):
        @pl.when(i + 1 < chunks)
        def _():
            own_weights(i + 1)

        @pl.when(i < chunks)
        def _():
            pass_on(i)

        @pl.when(i == 0)
        def _():
            for k in range(2, n, 2):
                token_arrival((u + n - k) % n).wait_recv()
                token_forward(k).start()
            for k in range(1, n, 2):
                token_arrival((u + n - k) % n).wait_recv()

        @pl.when(i + 1 < chunks)
        def _():
            for k in range(1, n):
                kv_copy(i + 1, k).start()

        @pl.when(i > 0)
        def _():
            c = i - 1
            across_arrived(c)
            for k in range(1, n):
                kv_arrival(c, k).wait_recv()
            attend(c)
            for k in range(1, n):
                out_copy(c, k).start()
            out_own(c).start()

        return carry

    lax.fori_loop(0, chunks + 1, chunk_step, 0)

    def drain(c, carry):
        weights_sent(c)
        for k in range(1, n):
            kv_copy(c, k).wait_send()
            out_copy(c, k).wait_send()
            out_arrival(c, k).wait_recv()
        out_own(c).wait()
        return carry

    lax.fori_loop(0, chunks, drain, 0)
    for k in range(2, n, 2):
        token_copy(k).wait_send()
        token_forward(k).wait_send()
    token_mate().wait_send()


def body(n, blocks, tokens, query_weight, key_values):
    seq_rows, depth = tokens.shape[1:]
    shard, heads, head_width = query_weight.shape
    all_heads = key_values.shape[2]
    width = heads * head_width
    chunk_heads = CHUNK_HEADS if heads % CHUNK_HEADS == 0 else 1
    chunks = heads // chunk_heads
    cols = width // chunks
    total_rows = n * seq_rows
    dma = pltpu.SemaphoreType.DMA
    flops = 2 * total_rows * width * (depth + 2 * total_rows)
    out = pl.pallas_call(
        functools.partial(kernel, n, blocks, head_width, chunks),
        out_shape=jax.ShapeDtypeStruct((seq_rows, all_heads * head_width), jnp.bfloat16),
        in_specs=[pl.BlockSpec(memory_space=pl.ANY)] * 3,
        out_specs=pl.BlockSpec(memory_space=pl.ANY),
        scratch_shapes=[
            pltpu.VMEM((total_rows, depth), jnp.bfloat16),
            pltpu.VMEM((depth, width), jnp.bfloat16),
            pltpu.VMEM((total_rows, 2 * width), jnp.bfloat16),
            pltpu.VMEM((total_rows, width), jnp.bfloat16),
            pltpu.VMEM((total_rows, cols), jnp.bfloat16),
            dma((3,)),
            dma((n,)),
            dma((n,)),
            dma((n,)),
            dma((3, chunks, blocks)),
            dma((chunks, blocks)),
            dma((chunks, n)),
            dma((chunks, n)),
            dma((chunks, n)),
            dma((chunks, n)),
            dma((chunks,)),
        ],
        compiler_params=pltpu.CompilerParams(
            collective_id=0, has_side_effects=True, vmem_limit_bytes=48 * 1024 * 1024
        ),
        cost_estimate=pl.CostEstimate(
            flops=flops,
            bytes_accessed=2 * (tokens.size + query_weight.size + key_values.size),
            transcendentals=total_rows * total_rows * heads,
        ),
    )(
        tokens[0],
        query_weight.reshape(shard, width),
        key_values[0].reshape(seq_rows, all_heads * 2 * head_width),
    )
    return out.reshape(1, seq_rows, all_heads, head_width)


def solution(mesh):
    return jax.shard_map(
        functools.partial(body, mesh.shape["uly"], mesh.shape["blk"]),
        mesh=mesh,
        in_specs=(P("blk", "uly", None), P("blk", "uly", None), P("blk", "uly", None, None)),
        out_specs=P("blk", "uly", None, None),
        check_vma=False,
    )
```

```python
import functools

import jax
import jax.numpy as jnp
from jax import lax
from jax.experimental import pallas as pl
from jax.experimental.pallas import tpu as pltpu
from jax.sharding import PartitionSpec as P

MESH = pl.DeviceIdType.MESH
CHUNK_HEADS = 1
AHEAD = 2
QUERY_ROWS = 256


def kernel(
    n,
    blocks,
    head_width,
    chunks,
    tok_in,
    w_in,
    kv_in,
    out_ref,
    tok,
    wbuf,
    kvbuf,
    att,
    qbuf,
    kv_raw,
    kv_wide,
    kv_flat,
    loc_sem,
    tok_send,
    tok_fwd,
    tok_recv,
    w_send,
    w_recv,
    side_send,
    side_recv,
    kv_send,
    kv_recv,
    out_send,
    out_recv,
    out_loc,
):
    u = lax.axis_index("uly")
    b = lax.axis_index("blk")
    line = blocks // 2
    z = b // 2
    y = b % 2
    mate = z * 2 + (1 - y)
    core_mate = u + 1 - 2 * (u % 2)
    seq_rows = tok_in.shape[0]
    shard = w_in.shape[0]
    width = w_in.shape[1]
    cols = width // chunks
    side = max(16, shard // 6 // 16 * 16)
    kv_width = 2 * width
    kv_cols = 2 * cols
    total_rows = n * seq_rows

    def ds(start, size):
        return pl.ds(pl.multiple_of(start * size, size), size)

    def remote(src, dst, send, recv, device):
        return pltpu.make_async_remote_copy(
            src_ref=src, dst_ref=dst, send_sem=send, recv_sem=recv,
            device_id=device, device_id_type=MESH,
        )

    has_up = z < line - 1
    has_down = z > 0

    raw_copy = pltpu.make_async_copy(kv_in, kv_raw, loc_sem.at[3])
    raw_copy.start()
    own_copies = (
        pltpu.make_async_copy(w_in, wbuf.at[ds(b, shard), :], loc_sem.at[0]),
        pltpu.make_async_copy(tok_in, tok.at[ds(u, seq_rows), :], loc_sem.at[1]),
    )
    for copy in own_copies:
        copy.start()

    barrier = pltpu.get_barrier_semaphore()

    def greet(device):
        pl.semaphore_signal(barrier, inc=1, device_id=device, device_id_type=MESH)

    for k in range(1, n):
        greet({"uly": (u + k) % n})
    greet({"blk": mate})

    @pl.when(has_up)
    def _():
        greet({"blk": b + 2})

    @pl.when(has_down)
    def _():
        greet({"blk": b - 2})

    inner = jnp.logical_and(has_up, has_down)

    @pl.when(inner)
    def _():
        pl.semaphore_wait(barrier, n + 2)

    @pl.when(jnp.logical_and(jnp.logical_not(inner), jnp.logical_or(has_up, has_down)))
    def _():
        pl.semaphore_wait(barrier, n + 1)

    @pl.when(jnp.logical_not(jnp.logical_or(has_up, has_down)))
    def _():
        pl.semaphore_wait(barrier, n)

    def piece(c, s):
        return wbuf.at[ds(s, shard), ds(c, cols)]

    UP, DOWN, ACROSS = 0, 1, 2

    def w_copy(c, s, way, own=False):
        step = (2, -2, 0)[way]
        device = mate if way == ACROSS else b + step
        src = w_in.at[:, ds(c, cols)] if own else piece(c, s)
        return remote(src, piece(c, s), w_send.at[way, c, s], w_recv.at[c, s], {"blk": device})

    def main_copy(c, s):
        rows = pl.ds(pl.multiple_of(s * shard + side, 16), shard - side)
        part = wbuf.at[rows, ds(c, cols)]
        return remote(part, part, w_send.at[ACROSS, c, s], w_recv.at[c, s], {"blk": mate})

    def side_copy(c, s, way):
        part = wbuf.at[pl.ds(pl.multiple_of(s * shard, 16), side), ds(c, cols)]
        device = b + (2, -2)[way]
        return remote(part, part, side_send.at[way, c, s], side_recv.at[c, s], {"blk": device})

    def own_weights(c):
        w_copy(c, b, ACROSS, True).start()

        @pl.when(has_up)
        def _():
            w_copy(c, b, UP, True).start()

        @pl.when(has_down)
        def _():
            w_copy(c, b, DOWN, True).start()

    def pass_on(c):
        ways = lambda d: (
            (UP, -2 * d, z - d >= 0, has_up),
            (DOWN, 2 * d, z + d < line, has_down),
        )

        def main(d):
            for way, step, there, more in ways(d):
                @pl.when(there)
                def _(way=way, step=step, more=more):
                    w_copy(c, b + step, ACROSS).wait_recv()

                    @pl.when(more)
                    def _():
                        w_copy(c, b + step, way).start()

                    main_copy(c, b + step).start()

        def sides(d):
            for way, step, there, more in ways(d):
                @pl.when(there)
                def _(way=way, step=step, more=more):
                    side_copy(c, mate + step, way).wait_recv()

                    @pl.when(more)
                    def _():
                        side_copy(c, mate + step, way).start()

        main(1)
        w_copy(c, mate, ACROSS).wait_recv()

        @pl.when(has_up)
        def _():
            side_copy(c, mate, UP).start()

        @pl.when(has_down)
        def _():
            side_copy(c, mate, DOWN).start()

        for d in range(2, line):
            main(d)
            sides(d - 1)
        sides(line - 1)

    def across_arrived(c):
        for j in range(line):
            @pl.when(j != z)
            def _():
                main_copy(c, 2 * j + 1 - y).wait_recv()

    def weights_sent(c):
        w_copy(c, b, ACROSS).wait_send()
        for j in range(line):
            s = 2 * j + y
            other = 2 * j + 1 - y

            @pl.when(j != z)
            def _():
                main_copy(c, s).wait_send()

            @pl.when(jnp.logical_and(has_up, j <= z))
            def _():
                w_copy(c, s, UP).wait_send()
                side_copy(c, other, UP).wait_send()

            @pl.when(jnp.logical_and(has_down, j >= z))
            def _():
                w_copy(c, s, DOWN).wait_send()
                side_copy(c, other, DOWN).wait_send()

    def token_rows(s):
        return tok.at[ds(s, seq_rows), :]

    def token_copy(k):
        return remote(tok_in, token_rows(u), tok_send.at[k], tok_recv.at[u], {"uly": (u + k) % n})

    def token_mate():
        return remote(tok_in, token_rows(u), tok_send.at[1], tok_recv.at[u], {"uly": core_mate})

    def token_forward(k):
        s = (u + n - k) % n
        return remote(token_rows(s), token_rows(s), tok_fwd.at[k], tok_recv.at[s], {"uly": core_mate})

    def token_arrival(s):
        return remote(token_rows(s), token_rows(s), tok_fwd.at[0], tok_recv.at[s], {"uly": core_mate})

    def kv_copy(c, k):
        to = (u + k) % n
        src = kv_flat.at[:, pl.ds(pl.multiple_of(to * kv_width + c * kv_cols, kv_cols), kv_cols)]
        dst = kvbuf.at[ds(u, seq_rows), ds(c, kv_cols)]
        return remote(src, dst, kv_send.at[c, k], kv_recv.at[c, u], {"uly": to})

    def kv_arrival(c, k):
        s = (u + n - k) % n
        dst = kvbuf.at[ds(s, seq_rows), ds(c, kv_cols)]
        return remote(dst, dst, kv_send.at[c, k], kv_recv.at[c, s], {"uly": s})

    def out_place(s, c):
        return out_ref.at[:, pl.ds(pl.multiple_of(s * width + c * cols, cols), cols)]

    def out_copy(c, k):
        to = (u + k) % n
        src = att.at[ds(to, seq_rows), ds(c, cols)]
        return remote(src, out_place(u, c), out_send.at[c, k], out_recv.at[c, u], {"uly": to})

    def out_arrival(c, k):
        s = (u + n - k) % n
        src = att.at[ds(s, seq_rows), ds(c, cols)]
        return remote(src, out_place(s, c), out_send.at[c, k], out_recv.at[c, s], {"uly": s})

    def out_own(c):
        return pltpu.make_async_copy(att.at[ds(u, seq_rows), ds(c, cols)], out_place(u, c), out_loc.at[c])

    for c in range(min(AHEAD, chunks)):
        own_weights(c)
    for k in range(2, n, 2):
        token_copy(k).start()
    token_mate().start()
    raw_copy.wait()

    heads = kv_in.shape[1]

    def widen(t, carry):
        part = kv_raw[ds(t, 16), :, :].astype(jnp.float32)
        for half in range(2):
            kv_wide[half, ds(t, 16 * heads), :] = part[
                :, :, half * head_width:(half + 1) * head_width
            ].reshape(16 * heads, head_width)
        return carry

    lax.fori_loop(0, seq_rows // 16, widen, 0)

    def gather_head(h, carry):
        for half in range(2):
            rows = kv_wide[half, pl.ds(h, seq_rows, stride=heads), :]
            kv_flat[:, ds(2 * h + half, head_width)] = rows.astype(jnp.bfloat16)
        return carry

    lax.fori_loop(0, heads, gather_head, 0)
    for k in range(1, n):
        kv_copy(0, k).start()
    own_kv = pltpu.make_async_copy(
        kv_flat.at[:, ds(u, kv_width)], kvbuf.at[ds(u, seq_rows), :], loc_sem.at[2]
    )
    own_kv.start()
    for copy in own_copies:
        copy.wait()
    own_kv.wait()

    scale = head_width ** (-0.5)
    block = min(QUERY_ROWS, total_rows)

    def attend(c):
        def rows_step(r, carry):
            rows = pl.ds(pl.multiple_of(r * block, block), block)
            qbuf[rows, :] = jnp.dot(
                tok[rows, :], wbuf[:, ds(c, cols)], preferred_element_type=jnp.float32
            ).astype(jnp.bfloat16)
            for h in range(cols // head_width):
                q = qbuf[rows, h * head_width:(h + 1) * head_width]
                at = c * kv_cols + 2 * h * head_width
                k = kvbuf[:, pl.ds(pl.multiple_of(at, head_width), head_width)]
                v = kvbuf[:, pl.ds(pl.multiple_of(at + head_width, head_width), head_width)]
                scores = lax.dot_general(
                    q, k, (((1,), (1,)), ((), ())), preferred_element_type=jnp.float32
                ) * scale
                soft = jnp.exp(scores - jnp.max(scores, axis=1, keepdims=True))
                row_sum = jnp.sum(soft, axis=1, keepdims=True)
                weighted = jnp.dot(
                    soft.astype(jnp.bfloat16), v, preferred_element_type=jnp.float32
                )
                place = pl.ds(pl.multiple_of(c * cols + h * head_width, head_width), head_width)
                att[rows, place] = (weighted / row_sum).astype(jnp.bfloat16)
            return carry

        lax.fori_loop(0, total_rows // block, rows_step, 0)

    def chunk_step(i, carry):
        @pl.when(i + AHEAD < chunks)
        def _():
            own_weights(i + AHEAD)

        @pl.when(i < chunks)
        def _():
            pass_on(i)

        @pl.when(i == 0)
        def _():
            for k in range(2, n, 2):
                token_arrival((u + n - k) % n).wait_recv()
                token_forward(k).start()
            for k in range(1, n, 2):
                token_arrival((u + n - k) % n).wait_recv()

        @pl.when(i + 1 < chunks)
        def _():
            for k in range(1, n):
                kv_copy(i + 1, k).start()

        @pl.when(i > 0)
        def _():
            c = i - 1
            across_arrived(c)
            for k in range(1, n):
                kv_arrival(c, k).wait_recv()
            attend(c)
            for k in range(1, n):
                out_copy(c, k).start()
            out_own(c).start()

        return carry

    lax.fori_loop(0, chunks + 1, chunk_step, 0)

    def drain(c, carry):
        weights_sent(c)
        for k in range(1, n):
            kv_copy(c, k).wait_send()
            out_copy(c, k).wait_send()
            out_arrival(c, k).wait_recv()
        out_own(c).wait()
        return carry

    lax.fori_loop(0, chunks, drain, 0)
    for k in range(2, n, 2):
        token_copy(k).wait_send()
        token_forward(k).wait_send()
    token_mate().wait_send()


def body(n, blocks, tokens, query_weight, key_values):
    seq_rows, depth = tokens.shape[1:]
    shard, heads, head_width = query_weight.shape
    all_heads = key_values.shape[2]
    width = heads * head_width
    chunk_heads = CHUNK_HEADS if heads % CHUNK_HEADS == 0 else 1
    chunks = heads // chunk_heads
    cols = width // chunks
    total_rows = n * seq_rows
    dma = pltpu.SemaphoreType.DMA
    flops = 2 * total_rows * width * (depth + 2 * total_rows)
    out = pl.pallas_call(
        functools.partial(kernel, n, blocks, head_width, chunks),
        out_shape=jax.ShapeDtypeStruct((seq_rows, all_heads * head_width), jnp.bfloat16),
        in_specs=[pl.BlockSpec(memory_space=pl.ANY)] * 3,
        out_specs=pl.BlockSpec(memory_space=pl.ANY),
        scratch_shapes=[
            pltpu.VMEM((total_rows, depth), jnp.bfloat16),
            pltpu.VMEM((depth, width), jnp.bfloat16),
            pltpu.VMEM((total_rows, 2 * width), jnp.bfloat16),
            pltpu.VMEM((total_rows, width), jnp.bfloat16),
            pltpu.VMEM((total_rows, cols), jnp.bfloat16),
            pltpu.VMEM((seq_rows, all_heads, 2 * head_width), jnp.bfloat16),
            pltpu.VMEM((2, seq_rows * all_heads, head_width), jnp.float32),
            pltpu.VMEM((seq_rows, all_heads * 2 * head_width), jnp.bfloat16),
            dma((4,)),
            dma((n,)),
            dma((n,)),
            dma((n,)),
            dma((3, chunks, blocks)),
            dma((chunks, blocks)),
            dma((2, chunks, blocks)),
            dma((chunks, blocks)),
            dma((chunks, n)),
            dma((chunks, n)),
            dma((chunks, n)),
            dma((chunks, n)),
            dma((chunks,)),
        ],
        compiler_params=pltpu.CompilerParams(
            collective_id=0, has_side_effects=True, vmem_limit_bytes=48 * 1024 * 1024
        ),
        cost_estimate=pl.CostEstimate(
            flops=flops,
            bytes_accessed=2 * (tokens.size + query_weight.size + key_values.size),
            transcendentals=total_rows * total_rows * heads,
        ),
    )(
        tokens[0],
        query_weight.reshape(shard, width),
        key_values[0],
    )
    return out.reshape(1, seq_rows, all_heads, head_width)


def solution(mesh):
    return jax.shard_map(
        functools.partial(body, mesh.shape["uly"], mesh.shape["blk"]),
        mesh=mesh,
        in_specs=(P("blk", "uly", None), P("blk", "uly", None), P("blk", "uly", None, None)),
        out_specs=P("blk", "uly", None, None),
        check_vma=False,
    )
```

```python
import functools

import jax
import jax.numpy as jnp
from jax import lax
from jax.experimental import pallas as pl
from jax.experimental.pallas import tpu as pltpu
from jax.sharding import PartitionSpec as P

MESH = pl.DeviceIdType.MESH
CHUNK_HEADS = 2
AHEAD = 1
QUERY_ROWS = 256


def kernel(
    n,
    blocks,
    head_width,
    chunks,
    tok_in,
    w_in,
    kv_in,
    out_ref,
    tok,
    wbuf,
    kvbuf,
    att,
    qbuf,
    loc_sem,
    tok_send,
    tok_fwd,
    tok_recv,
    w_send,
    w_recv,
    side_send,
    side_recv,
    kv_send,
    kv_recv,
    out_send,
    out_recv,
    out_loc,
):
    u = lax.axis_index("uly")
    b = lax.axis_index("blk")
    line = blocks // 2
    z = b // 2
    y = b % 2
    mate = z * 2 + (1 - y)
    core_mate = u + 1 - 2 * (u % 2)
    seq_rows = tok_in.shape[0]
    shard = w_in.shape[1]
    heads = w_in.shape[0]
    chunk_heads = heads // chunks
    side = max(16, shard // 6 // 16 * 16)
    total_rows = n * seq_rows

    def ds(start, size):
        return pl.ds(pl.multiple_of(start * size, size), size)

    def remote(src, dst, send, recv, device):
        return pltpu.make_async_remote_copy(
            src_ref=src, dst_ref=dst, send_sem=send, recv_sem=recv,
            device_id=device, device_id_type=MESH,
        )

    has_up = z < line - 1
    has_down = z > 0

    own_copies = (
        pltpu.make_async_copy(w_in, wbuf.at[:, ds(b, shard), :], loc_sem.at[0]),
        pltpu.make_async_copy(tok_in, tok.at[ds(u, seq_rows), :], loc_sem.at[1]),
        pltpu.make_async_copy(
            kv_in.at[ds(u, heads)], kvbuf.at[:, ds(u, seq_rows), :], loc_sem.at[2]
        ),
    )
    for copy in own_copies:
        copy.start()

    barrier = pltpu.get_barrier_semaphore()

    def greet(device):
        pl.semaphore_signal(barrier, inc=1, device_id=device, device_id_type=MESH)

    for k in range(1, n):
        greet({"uly": (u + k) % n})
    greet({"blk": mate})

    @pl.when(has_up)
    def _():
        greet({"blk": b + 2})

    @pl.when(has_down)
    def _():
        greet({"blk": b - 2})

    inner = jnp.logical_and(has_up, has_down)

    @pl.when(inner)
    def _():
        pl.semaphore_wait(barrier, n + 2)

    @pl.when(jnp.logical_and(jnp.logical_not(inner), jnp.logical_or(has_up, has_down)))
    def _():
        pl.semaphore_wait(barrier, n + 1)

    @pl.when(jnp.logical_not(jnp.logical_or(has_up, has_down)))
    def _():
        pl.semaphore_wait(barrier, n)

    def piece(c, s):
        return wbuf.at[ds(c, chunk_heads), ds(s, shard), :]

    UP, DOWN, ACROSS = 0, 1, 2

    def w_copy(c, s, way, own=False):
        step = (2, -2, 0)[way]
        device = mate if way == ACROSS else b + step
        src = w_in.at[ds(c, chunk_heads)] if own else piece(c, s)
        return remote(src, piece(c, s), w_send.at[way, c, s], w_recv.at[c, s], {"blk": device})

    def main_copy(c, s):
        rows = pl.ds(pl.multiple_of(s * shard + side, 16), shard - side)
        part = wbuf.at[ds(c, chunk_heads), rows, :]
        return remote(part, part, w_send.at[ACROSS, c, s], w_recv.at[c, s], {"blk": mate})

    def side_copy(c, s, way):
        part = wbuf.at[
            ds(c, chunk_heads), pl.ds(pl.multiple_of(s * shard, 16), side), :
        ]
        device = b + (2, -2)[way]
        return remote(part, part, side_send.at[way, c, s], side_recv.at[c, s], {"blk": device})

    def own_weights(c):
        w_copy(c, b, ACROSS, True).start()

        @pl.when(has_up)
        def _():
            w_copy(c, b, UP, True).start()

        @pl.when(has_down)
        def _():
            w_copy(c, b, DOWN, True).start()

    def pass_on(c):
        ways = lambda d: (
            (UP, -2 * d, z - d >= 0, has_up),
            (DOWN, 2 * d, z + d < line, has_down),
        )

        def main(d):
            for way, step, there, more in ways(d):
                @pl.when(there)
                def _(way=way, step=step, more=more):
                    w_copy(c, b + step, ACROSS).wait_recv()

                    @pl.when(more)
                    def _():
                        w_copy(c, b + step, way).start()

                    main_copy(c, b + step).start()

        def sides(d):
            for way, step, there, more in ways(d):
                @pl.when(there)
                def _(way=way, step=step, more=more):
                    side_copy(c, mate + step, way).wait_recv()

                    @pl.when(more)
                    def _():
                        side_copy(c, mate + step, way).start()

        main(1)
        w_copy(c, mate, ACROSS).wait_recv()

        @pl.when(has_up)
        def _():
            side_copy(c, mate, UP).start()

        @pl.when(has_down)
        def _():
            side_copy(c, mate, DOWN).start()

        for d in range(2, line):
            main(d)
            sides(d - 1)
        sides(line - 1)

    def across_arrived(c):
        for j in range(line):
            @pl.when(j != z)
            def _():
                main_copy(c, 2 * j + 1 - y).wait_recv()

    def weights_sent(c):
        w_copy(c, b, ACROSS).wait_send()
        for j in range(line):
            s = 2 * j + y
            other = 2 * j + 1 - y

            @pl.when(j != z)
            def _():
                main_copy(c, s).wait_send()

            @pl.when(jnp.logical_and(has_up, j <= z))
            def _():
                w_copy(c, s, UP).wait_send()
                side_copy(c, other, UP).wait_send()

            @pl.when(jnp.logical_and(has_down, j >= z))
            def _():
                w_copy(c, s, DOWN).wait_send()
                side_copy(c, other, DOWN).wait_send()

    def token_rows(s):
        return tok.at[ds(s, seq_rows), :]

    def token_copy(k):
        return remote(tok_in, token_rows(u), tok_send.at[k], tok_recv.at[u], {"uly": (u + k) % n})

    def token_mate():
        return remote(tok_in, token_rows(u), tok_send.at[1], tok_recv.at[u], {"uly": core_mate})

    def token_forward(k):
        s = (u + n - k) % n
        return remote(token_rows(s), token_rows(s), tok_fwd.at[k], tok_recv.at[s], {"uly": core_mate})

    def token_arrival(s):
        return remote(token_rows(s), token_rows(s), tok_fwd.at[0], tok_recv.at[s], {"uly": core_mate})

    def kv_copy(c, k):
        to = (u + k) % n
        src = kv_in.at[pl.ds(to * heads + c * chunk_heads, chunk_heads)]
        dst = kvbuf.at[ds(c, chunk_heads), ds(u, seq_rows), :]
        return remote(src, dst, kv_send.at[c, k], kv_recv.at[c, u], {"uly": to})

    def kv_arrival(c, k):
        s = (u + n - k) % n
        dst = kvbuf.at[ds(c, chunk_heads), ds(s, seq_rows), :]
        return remote(dst, dst, kv_send.at[c, k], kv_recv.at[c, s], {"uly": s})

    def out_place(s, c):
        return out_ref.at[pl.ds(s * heads + c * chunk_heads, chunk_heads)]

    def out_copy(c, k):
        to = (u + k) % n
        src = att.at[ds(c, chunk_heads), ds(to, seq_rows), :]
        return remote(src, out_place(u, c), out_send.at[c, k], out_recv.at[c, u], {"uly": to})

    def out_arrival(c, k):
        s = (u + n - k) % n
        src = att.at[ds(c, chunk_heads), ds(s, seq_rows), :]
        return remote(src, out_place(s, c), out_send.at[c, k], out_recv.at[c, s], {"uly": s})

    def out_own(c):
        return pltpu.make_async_copy(att.at[ds(c, chunk_heads), ds(u, seq_rows), :], out_place(u, c), out_loc.at[c])

    for c in range(min(AHEAD, chunks)):
        own_weights(c)
    for k in range(2, n, 2):
        token_copy(k).start()
    token_mate().start()
    for k in range(1, n):
        kv_copy(0, k).start()
    for copy in own_copies:
        copy.wait()

    scale = head_width ** (-0.5)
    block = min(QUERY_ROWS, total_rows)

    def attend(c):
        def rows_step(r, carry):
            rows = pl.ds(pl.multiple_of(r * block, block), block)
            weight = jnp.concatenate(
                [wbuf[c * chunk_heads + h, :, :] for h in range(chunk_heads)], axis=1
            )
            qbuf[rows, :] = jnp.dot(
                tok[rows, :], weight, preferred_element_type=jnp.float32
            ).astype(jnp.bfloat16)
            for h in range(chunk_heads):
                q = qbuf[rows, h * head_width:(h + 1) * head_width]
                at = c * chunk_heads + h
                k = kvbuf[at, :, :head_width]
                v = kvbuf[at, :, head_width:]
                scores = lax.dot_general(
                    q, k, (((1,), (1,)), ((), ())), preferred_element_type=jnp.float32
                ) * scale
                soft = jnp.exp(scores - jnp.max(scores, axis=1, keepdims=True))
                row_sum = jnp.sum(soft, axis=1, keepdims=True)
                weighted = jnp.dot(
                    soft.astype(jnp.bfloat16), v, preferred_element_type=jnp.float32
                )
                att[at, rows, :] = (weighted / row_sum).astype(jnp.bfloat16)
            return carry

        lax.fori_loop(0, total_rows // block, rows_step, 0)

    def chunk_step(i, carry):
        @pl.when(i + AHEAD < chunks)
        def _():
            own_weights(i + AHEAD)

        @pl.when(i < chunks)
        def _():
            pass_on(i)

        @pl.when(i == 0)
        def _():
            for k in range(2, n, 2):
                token_arrival((u + n - k) % n).wait_recv()
                token_forward(k).start()
            for k in range(1, n, 2):
                token_arrival((u + n - k) % n).wait_recv()

        @pl.when(i + 1 < chunks)
        def _():
            for k in range(1, n):
                kv_copy(i + 1, k).start()

        @pl.when(i > 0)
        def _():
            c = i - 1
            across_arrived(c)
            for k in range(1, n):
                kv_arrival(c, k).wait_recv()
            attend(c)
            for k in range(1, n):
                out_copy(c, k).start()
            out_own(c).start()

        return carry

    lax.fori_loop(0, chunks + 1, chunk_step, 0)

    def drain(c, carry):
        weights_sent(c)
        for k in range(1, n):
            kv_copy(c, k).wait_send()
            out_copy(c, k).wait_send()
            out_arrival(c, k).wait_recv()
        out_own(c).wait()
        return carry

    lax.fori_loop(0, chunks, drain, 0)
    for k in range(2, n, 2):
        token_copy(k).wait_send()
        token_forward(k).wait_send()
    token_mate().wait_send()


def body(n, blocks, tokens, query_weight, key_values):
    seq_rows, depth = tokens.shape[1:]
    shard, heads, head_width = query_weight.shape
    all_heads = key_values.shape[2]
    width = heads * head_width
    chunk_heads = CHUNK_HEADS if heads % CHUNK_HEADS == 0 else 1
    chunks = heads // chunk_heads
    cols = width // chunks
    total_rows = n * seq_rows
    dma = pltpu.SemaphoreType.DMA
    flops = 2 * total_rows * width * (depth + 2 * total_rows)
    out = pl.pallas_call(
        functools.partial(kernel, n, blocks, head_width, chunks),
        out_shape=jax.ShapeDtypeStruct((all_heads, seq_rows, head_width), jnp.bfloat16),
        in_specs=[pl.BlockSpec(memory_space=pl.ANY)] * 3,
        out_specs=pl.BlockSpec(memory_space=pl.ANY),
        scratch_shapes=[
            pltpu.VMEM((total_rows, depth), jnp.bfloat16),
            pltpu.VMEM((heads, depth, head_width), jnp.bfloat16),
            pltpu.VMEM((heads, total_rows, 2 * head_width), jnp.bfloat16),
            pltpu.VMEM((heads, total_rows, head_width), jnp.bfloat16),
            pltpu.VMEM((total_rows, cols), jnp.bfloat16),
            dma((3,)),
            dma((n,)),
            dma((n,)),
            dma((n,)),
            dma((3, chunks, blocks)),
            dma((chunks, blocks)),
            dma((2, chunks, blocks)),
            dma((chunks, blocks)),
            dma((chunks, n)),
            dma((chunks, n)),
            dma((chunks, n)),
            dma((chunks, n)),
            dma((chunks,)),
        ],
        compiler_params=pltpu.CompilerParams(
            collective_id=0, has_side_effects=True, vmem_limit_bytes=48 * 1024 * 1024
        ),
        cost_estimate=pl.CostEstimate(
            flops=flops,
            bytes_accessed=2 * (tokens.size + query_weight.size + key_values.size),
            transcendentals=total_rows * total_rows * heads,
        ),
    )(
        tokens[0],
        jnp.transpose(query_weight, (1, 0, 2)),
        jnp.transpose(key_values[0], (1, 0, 2)),
    )
    return jnp.transpose(out, (1, 0, 2))[None]


def solution(mesh):
    return jax.shard_map(
        functools.partial(body, mesh.shape["uly"], mesh.shape["blk"]),
        mesh=mesh,
        in_specs=(P("blk", "uly", None), P("blk", "uly", None), P("blk", "uly", None, None)),
        out_specs=P("blk", "uly", None, None),
        check_vma=False,
    )
```

```python
import functools

import jax
import jax.numpy as jnp
from jax import lax
from jax.experimental import pallas as pl
from jax.experimental.pallas import tpu as pltpu
from jax.sharding import PartitionSpec as P

MESH = pl.DeviceIdType.MESH
CHUNK_HEADS = 2
AHEAD = 2
LAG = 2
QUERY_ROWS = 256


def kernel(
    n,
    blocks,
    head_width,
    chunks,
    tok_in,
    w_in,
    kv_in,
    out_ref,
    tok,
    wbuf,
    kvbuf,
    att,
    qbuf,
    loc_sem,
    tok_send,
    tok_fwd,
    tok_recv,
    w_send,
    w_recv,
    side_send,
    side_recv,
    kv_send,
    kv_recv,
    out_send,
    out_recv,
    out_loc,
):
    u = lax.axis_index("uly")
    b = lax.axis_index("blk")
    line = blocks // 2
    z = b // 2
    y = b % 2
    mate = z * 2 + (1 - y)
    core_mate = u + 1 - 2 * (u % 2)
    seq_rows = tok_in.shape[0]
    shard = w_in.shape[1]
    heads = w_in.shape[0]
    chunk_heads = heads // chunks
    side = max(16, shard // 6 // 16 * 16)
    total_rows = n * seq_rows

    def ds(start, size):
        return pl.ds(pl.multiple_of(start * size, size), size)

    def remote(src, dst, send, recv, device):
        return pltpu.make_async_remote_copy(
            src_ref=src, dst_ref=dst, send_sem=send, recv_sem=recv,
            device_id=device, device_id_type=MESH,
        )

    has_up = z < line - 1
    has_down = z > 0

    own_copies = (
        pltpu.make_async_copy(w_in, wbuf.at[:, ds(b, shard), :], loc_sem.at[0]),
        pltpu.make_async_copy(tok_in, tok.at[ds(u, seq_rows), :], loc_sem.at[1]),
        pltpu.make_async_copy(
            kv_in.at[ds(u, heads)], kvbuf.at[:, ds(u, seq_rows), :], loc_sem.at[2]
        ),
    )
    for copy in own_copies:
        copy.start()

    barrier = pltpu.get_barrier_semaphore()

    def greet(device):
        pl.semaphore_signal(barrier, inc=1, device_id=device, device_id_type=MESH)

    for k in range(1, n):
        greet({"uly": (u + k) % n})
    greet({"blk": mate})

    @pl.when(has_up)
    def _():
        greet({"blk": b + 2})

    @pl.when(has_down)
    def _():
        greet({"blk": b - 2})

    inner = jnp.logical_and(has_up, has_down)

    @pl.when(inner)
    def _():
        pl.semaphore_wait(barrier, n + 2)

    @pl.when(jnp.logical_and(jnp.logical_not(inner), jnp.logical_or(has_up, has_down)))
    def _():
        pl.semaphore_wait(barrier, n + 1)

    @pl.when(jnp.logical_not(jnp.logical_or(has_up, has_down)))
    def _():
        pl.semaphore_wait(barrier, n)

    def piece(c, s):
        return wbuf.at[ds(c, chunk_heads), ds(s, shard), :]

    UP, DOWN, ACROSS = 0, 1, 2

    def w_copy(c, s, way, own=False):
        step = (2, -2, 0)[way]
        device = mate if way == ACROSS else b + step
        src = w_in.at[ds(c, chunk_heads)] if own else piece(c, s)
        return remote(src, piece(c, s), w_send.at[way, c, s], w_recv.at[c, s], {"blk": device})

    def main_copy(c, s):
        rows = pl.ds(pl.multiple_of(s * shard + side, 16), shard - side)
        part = wbuf.at[ds(c, chunk_heads), rows, :]
        return remote(part, part, w_send.at[ACROSS, c, s], w_recv.at[c, s], {"blk": mate})

    def side_copy(c, s, way):
        part = wbuf.at[
            ds(c, chunk_heads), pl.ds(pl.multiple_of(s * shard, 16), side), :
        ]
        device = b + (2, -2)[way]
        return remote(part, part, side_send.at[way, c, s], side_recv.at[c, s], {"blk": device})

    def own_weights(c):
        w_copy(c, b, ACROSS, True).start()

        @pl.when(has_up)
        def _():
            w_copy(c, b, UP, True).start()

        @pl.when(has_down)
        def _():
            w_copy(c, b, DOWN, True).start()

    def pass_on(c, between):
        ways = lambda d: (
            (UP, -2 * d, z - d >= 0, has_up),
            (DOWN, 2 * d, z + d < line, has_down),
        )

        def main(d):
            for way, step, there, more in ways(d):
                @pl.when(there)
                def _(way=way, step=step, more=more):
                    w_copy(c, b + step, ACROSS).wait_recv()

                    @pl.when(more)
                    def _():
                        w_copy(c, b + step, way).start()

                    main_copy(c, b + step).start()

        def sides(d):
            for way, step, there, more in ways(d):
                @pl.when(there)
                def _(way=way, step=step, more=more):
                    side_copy(c, mate + step, way).wait_recv()

                    @pl.when(more)
                    def _():
                        side_copy(c, mate + step, way).start()

        def forward(*steps):
            @pl.when(c < chunks)
            def _():
                for step in steps:
                    step()

        def first():
            w_copy(c, mate, ACROSS).wait_recv()

            @pl.when(has_up)
            def _():
                side_copy(c, mate, UP).start()

            @pl.when(has_down)
            def _():
                side_copy(c, mate, DOWN).start()

        forward(functools.partial(main, 1), first)
        for d in range(2, line):
            if between:
                between.pop(0)()
            forward(functools.partial(main, d), functools.partial(sides, d - 1))
        if between:
            between.pop(0)()
        forward(lambda: sides(line - 1))
        for unit in between:
            unit()

    def across_arrived(c):
        for j in range(line):
            @pl.when(j != z)
            def _():
                main_copy(c, 2 * j + 1 - y).wait_recv()

    def weights_sent(c):
        w_copy(c, b, ACROSS).wait_send()
        for j in range(line):
            s = 2 * j + y
            other = 2 * j + 1 - y

            @pl.when(j != z)
            def _():
                main_copy(c, s).wait_send()

            @pl.when(jnp.logical_and(has_up, j <= z))
            def _():
                w_copy(c, s, UP).wait_send()
                side_copy(c, other, UP).wait_send()

            @pl.when(jnp.logical_and(has_down, j >= z))
            def _():
                w_copy(c, s, DOWN).wait_send()
                side_copy(c, other, DOWN).wait_send()

    def token_rows(s):
        return tok.at[ds(s, seq_rows), :]

    def token_copy(k):
        return remote(tok_in, token_rows(u), tok_send.at[k], tok_recv.at[u], {"uly": (u + k) % n})

    def token_mate():
        return remote(tok_in, token_rows(u), tok_send.at[1], tok_recv.at[u], {"uly": core_mate})

    def token_forward(k):
        s = (u + n - k) % n
        return remote(token_rows(s), token_rows(s), tok_fwd.at[k], tok_recv.at[s], {"uly": core_mate})

    def token_arrival(s):
        return remote(token_rows(s), token_rows(s), tok_fwd.at[0], tok_recv.at[s], {"uly": core_mate})

    def kv_copy(c, k):
        to = (u + k) % n
        src = kv_in.at[pl.ds(to * heads + c * chunk_heads, chunk_heads)]
        dst = kvbuf.at[ds(c, chunk_heads), ds(u, seq_rows), :]
        return remote(src, dst, kv_send.at[c, k], kv_recv.at[c, u], {"uly": to})

    def kv_arrival(c, k):
        s = (u + n - k) % n
        dst = kvbuf.at[ds(c, chunk_heads), ds(s, seq_rows), :]
        return remote(dst, dst, kv_send.at[c, k], kv_recv.at[c, s], {"uly": s})

    def out_place(s, c):
        return out_ref.at[pl.ds(s * heads + c * chunk_heads, chunk_heads)]

    def out_copy(c, k):
        to = (u + k) % n
        src = att.at[ds(c, chunk_heads), ds(to, seq_rows), :]
        return remote(src, out_place(u, c), out_send.at[c, k], out_recv.at[c, u], {"uly": to})

    def out_arrival(c, k):
        s = (u + n - k) % n
        src = att.at[ds(c, chunk_heads), ds(s, seq_rows), :]
        return remote(src, out_place(s, c), out_send.at[c, k], out_recv.at[c, s], {"uly": s})

    def out_own(c):
        return pltpu.make_async_copy(att.at[ds(c, chunk_heads), ds(u, seq_rows), :], out_place(u, c), out_loc.at[c])

    for c in range(min(AHEAD, chunks)):
        own_weights(c)
    for k in range(2, n, 2):
        token_copy(k).start()
    token_mate().start()
    for k in range(1, n):
        kv_copy(0, k).start()
    for copy in own_copies:
        copy.wait()

    scale = head_width ** (-0.5)
    block = min(QUERY_ROWS, total_rows)

    def project(c):
        weight = jnp.concatenate(
            [wbuf[c * chunk_heads + h, :, :] for h in range(chunk_heads)], axis=1
        )
        if total_rows <= 512:
            qbuf[...] = jnp.dot(
                tok[...], weight, preferred_element_type=jnp.float32
            ).astype(jnp.bfloat16)
        else:
            def rows_step(r, carry):
                rows = ds(r, block)
                qbuf[rows, :] = jnp.dot(
                    tok[rows, :], weight, preferred_element_type=jnp.float32
                ).astype(jnp.bfloat16)
                return carry

            lax.fori_loop(0, total_rows // block, rows_step, 0)

    def attend(c, h):
        at = c * chunk_heads + h

        def rows_step(r, carry):
            rows = ds(r, block)
            q = qbuf[rows, h * head_width:(h + 1) * head_width]
            k = kvbuf[at, :, :head_width]
            v = kvbuf[at, :, head_width:]
            scores = lax.dot_general(
                q, k, (((1,), (1,)), ((), ())), preferred_element_type=jnp.float32
            ) * scale
            soft = jnp.exp(scores - jnp.max(scores, axis=1, keepdims=True))
            row_sum = jnp.sum(soft, axis=1, keepdims=True)
            weighted = jnp.dot(soft.astype(jnp.bfloat16), v, preferred_element_type=jnp.float32)
            att[at, rows, :] = (weighted / row_sum).astype(jnp.bfloat16)
            return carry

        lax.fori_loop(0, total_rows // block, rows_step, 0)

    def chunk_step(i, carry):
        c = i - LAG

        def unit(*steps):
            def run():
                @pl.when(c >= 0)
                def _():
                    for step in steps:
                        step()

            return run

        def ready():
            across_arrived(c)
            for k in range(1, n):
                kv_arrival(c, k).wait_recv()

        def give_back():
            for k in range(1, n):
                out_copy(c, k).start()
            out_own(c).start()

        units = [unit(ready, lambda: project(c))]
        for h in range(chunk_heads):
            units.append(unit(functools.partial(attend, c, h)))

        @pl.when(i + AHEAD < chunks)
        def _():
            own_weights(i + AHEAD)

        pass_on(i, units)
        unit(give_back)()

        @pl.when(i == 1)
        def _():
            for k in range(2, n, 2):
                token_arrival((u + n - k) % n).wait_recv()
                token_forward(k).start()
            for k in range(1, n, 2):
                token_arrival((u + n - k) % n).wait_recv()

        @pl.when(i + 1 < chunks)
        def _():
            for k in range(1, n):
                kv_copy(i + 1, k).start()

        return carry

    lax.fori_loop(0, chunks + LAG, chunk_step, 0)

    def drain(c, carry):
        weights_sent(c)
        for k in range(1, n):
            kv_copy(c, k).wait_send()
            out_copy(c, k).wait_send()
            out_arrival(c, k).wait_recv()
        out_own(c).wait()
        return carry

    lax.fori_loop(0, chunks, drain, 0)
    for k in range(2, n, 2):
        token_copy(k).wait_send()
        token_forward(k).wait_send()
    token_mate().wait_send()


def body(n, blocks, tokens, query_weight, key_values):
    seq_rows, depth = tokens.shape[1:]
    shard, heads, head_width = query_weight.shape
    all_heads = key_values.shape[2]
    width = heads * head_width
    chunk_heads = CHUNK_HEADS if heads % CHUNK_HEADS == 0 else 1
    chunks = heads // chunk_heads
    cols = width // chunks
    total_rows = n * seq_rows
    dma = pltpu.SemaphoreType.DMA
    flops = 2 * total_rows * width * (depth + 2 * total_rows)
    out = pl.pallas_call(
        functools.partial(kernel, n, blocks, head_width, chunks),
        out_shape=jax.ShapeDtypeStruct((all_heads, seq_rows, head_width), jnp.bfloat16),
        in_specs=[pl.BlockSpec(memory_space=pl.ANY)] * 3,
        out_specs=pl.BlockSpec(memory_space=pl.ANY),
        scratch_shapes=[
            pltpu.VMEM((total_rows, depth), jnp.bfloat16),
            pltpu.VMEM((heads, depth, head_width), jnp.bfloat16),
            pltpu.VMEM((heads, total_rows, 2 * head_width), jnp.bfloat16),
            pltpu.VMEM((heads, total_rows, head_width), jnp.bfloat16),
            pltpu.VMEM((total_rows, cols), jnp.bfloat16),
            dma((3,)),
            dma((n,)),
            dma((n,)),
            dma((n,)),
            dma((3, chunks, blocks)),
            dma((chunks, blocks)),
            dma((2, chunks, blocks)),
            dma((chunks, blocks)),
            dma((chunks, n)),
            dma((chunks, n)),
            dma((chunks, n)),
            dma((chunks, n)),
            dma((chunks,)),
        ],
        compiler_params=pltpu.CompilerParams(
            collective_id=0, has_side_effects=True, vmem_limit_bytes=48 * 1024 * 1024
        ),
        cost_estimate=pl.CostEstimate(
            flops=flops,
            bytes_accessed=2 * (tokens.size + query_weight.size + key_values.size),
            transcendentals=total_rows * total_rows * heads,
        ),
    )(
        tokens[0],
        jnp.transpose(query_weight, (1, 0, 2)),
        jnp.transpose(key_values[0], (1, 0, 2)),
    )
    return jnp.transpose(out, (1, 0, 2))[None]


def solution(mesh):
    return jax.shard_map(
        functools.partial(body, mesh.shape["uly"], mesh.shape["blk"]),
        mesh=mesh,
        in_specs=(P("blk", "uly", None), P("blk", "uly", None), P("blk", "uly", None, None)),
        out_specs=P("blk", "uly", None, None),
        check_vma=False,
    )
```

```python
import functools

import jax
import jax.numpy as jnp
from jax import lax
from jax.experimental import pallas as pl
from jax.experimental.pallas import tpu as pltpu
from jax.sharding import PartitionSpec as P

MESH = pl.DeviceIdType.MESH
CHUNK_HEADS = 2
AHEAD = 2
LAG = 1
QUERY_ROWS = 256


def kernel(
    n,
    blocks,
    head_width,
    chunks,
    tok_in,
    w_in,
    kv_in,
    out_ref,
    tok,
    wbuf,
    kvbuf,
    att,
    qbuf,
    loc_sem,
    tok_send,
    tok_fwd,
    tok_recv,
    w_send,
    w_recv,
    side_send,
    side_recv,
    kv_send,
    kv_recv,
    out_send,
    out_recv,
    out_loc,
):
    u = lax.axis_index("uly")
    b = lax.axis_index("blk")
    line = blocks // 2
    z = b // 2
    y = b % 2
    mate = z * 2 + (1 - y)
    core_mate = u + 1 - 2 * (u % 2)
    seq_rows = tok_in.shape[0]
    shard = w_in.shape[1]
    heads = w_in.shape[0]
    chunk_heads = heads // chunks
    side = max(16, shard // 6 // 16 * 16)
    total_rows = n * seq_rows

    def ds(start, size):
        return pl.ds(pl.multiple_of(start * size, size), size)

    def remote(src, dst, send, recv, device):
        return pltpu.make_async_remote_copy(
            src_ref=src, dst_ref=dst, send_sem=send, recv_sem=recv,
            device_id=device, device_id_type=MESH,
        )

    has_up = z < line - 1
    has_down = z > 0

    own_copies = (
        pltpu.make_async_copy(w_in, wbuf.at[:, ds(b, shard), :], loc_sem.at[0]),
        pltpu.make_async_copy(tok_in, tok.at[ds(u, seq_rows), :], loc_sem.at[1]),
        pltpu.make_async_copy(
            kv_in.at[ds(u, heads)], kvbuf.at[:, ds(u, seq_rows), :], loc_sem.at[2]
        ),
    )
    for copy in own_copies:
        copy.start()

    barrier = pltpu.get_barrier_semaphore()

    def greet(device):
        pl.semaphore_signal(barrier, inc=1, device_id=device, device_id_type=MESH)

    for k in range(1, n):
        greet({"uly": (u + k) % n})
    greet({"blk": mate})

    @pl.when(has_up)
    def _():
        greet({"blk": b + 2})

    @pl.when(has_down)
    def _():
        greet({"blk": b - 2})

    inner = jnp.logical_and(has_up, has_down)

    @pl.when(inner)
    def _():
        pl.semaphore_wait(barrier, n + 2)

    @pl.when(jnp.logical_and(jnp.logical_not(inner), jnp.logical_or(has_up, has_down)))
    def _():
        pl.semaphore_wait(barrier, n + 1)

    @pl.when(jnp.logical_not(jnp.logical_or(has_up, has_down)))
    def _():
        pl.semaphore_wait(barrier, n)

    def piece(c, s):
        return wbuf.at[ds(c, chunk_heads), ds(s, shard), :]

    UP, DOWN, ACROSS = 0, 1, 2

    def w_copy(c, s, way, own=False):
        step = (2, -2, 0)[way]
        device = mate if way == ACROSS else b + step
        src = w_in.at[ds(c, chunk_heads)] if own else piece(c, s)
        return remote(src, piece(c, s), w_send.at[way, c, s], w_recv.at[c, s], {"blk": device})

    def main_copy(c, s):
        rows = pl.ds(pl.multiple_of(s * shard + side, 16), shard - side)
        part = wbuf.at[ds(c, chunk_heads), rows, :]
        return remote(part, part, w_send.at[ACROSS, c, s], w_recv.at[c, s], {"blk": mate})

    def side_copy(c, s, way):
        part = wbuf.at[
            ds(c, chunk_heads), pl.ds(pl.multiple_of(s * shard, 16), side), :
        ]
        device = b + (2, -2)[way]
        return remote(part, part, side_send.at[way, c, s], side_recv.at[c, s], {"blk": device})

    def own_weights(c):
        w_copy(c, b, ACROSS, True).start()

        @pl.when(has_up)
        def _():
            w_copy(c, b, UP, True).start()

        @pl.when(has_down)
        def _():
            w_copy(c, b, DOWN, True).start()

    def pass_on(c, between):
        ways = lambda d: (
            (UP, -2 * d, z - d >= 0, has_up),
            (DOWN, 2 * d, z + d < line, has_down),
        )

        def main(d):
            for way, step, there, more in ways(d):
                @pl.when(there)
                def _(way=way, step=step, more=more):
                    w_copy(c, b + step, ACROSS).wait_recv()

                    @pl.when(more)
                    def _():
                        w_copy(c, b + step, way).start()

                    main_copy(c, b + step).start()

        def sides(d):
            for way, step, there, more in ways(d):
                @pl.when(there)
                def _(way=way, step=step, more=more):
                    side_copy(c, mate + step, way).wait_recv()

                    @pl.when(more)
                    def _():
                        side_copy(c, mate + step, way).start()

        def forward(*steps):
            @pl.when(c < chunks)
            def _():
                for step in steps:
                    step()

        def first():
            w_copy(c, mate, ACROSS).wait_recv()

            @pl.when(has_up)
            def _():
                side_copy(c, mate, UP).start()

            @pl.when(has_down)
            def _():
                side_copy(c, mate, DOWN).start()

        forward(functools.partial(main, 1), first)
        for d in range(2, line):
            if between:
                between.pop(0)()
            forward(functools.partial(main, d), functools.partial(sides, d - 1))
        if between:
            between.pop(0)()
        forward(lambda: sides(line - 1))
        for unit in between:
            unit()

    def across_arrived(c):
        for j in range(line):
            @pl.when(j != z)
            def _():
                main_copy(c, 2 * j + 1 - y).wait_recv()

    def weights_sent(c):
        w_copy(c, b, ACROSS).wait_send()
        for j in range(line):
            s = 2 * j + y
            other = 2 * j + 1 - y

            @pl.when(j != z)
            def _():
                main_copy(c, s).wait_send()

            @pl.when(jnp.logical_and(has_up, j <= z))
            def _():
                w_copy(c, s, UP).wait_send()
                side_copy(c, other, UP).wait_send()

            @pl.when(jnp.logical_and(has_down, j >= z))
            def _():
                w_copy(c, s, DOWN).wait_send()
                side_copy(c, other, DOWN).wait_send()

    def token_rows(s):
        return tok.at[ds(s, seq_rows), :]

    def token_copy(k):
        return remote(tok_in, token_rows(u), tok_send.at[k], tok_recv.at[u], {"uly": (u + k) % n})

    def token_mate():
        return remote(tok_in, token_rows(u), tok_send.at[1], tok_recv.at[u], {"uly": core_mate})

    def token_forward(k):
        s = (u + n - k) % n
        return remote(token_rows(s), token_rows(s), tok_fwd.at[k], tok_recv.at[s], {"uly": core_mate})

    def token_arrival(s):
        return remote(token_rows(s), token_rows(s), tok_fwd.at[0], tok_recv.at[s], {"uly": core_mate})

    def kv_copy(c, k):
        to = (u + k) % n
        src = kv_in.at[pl.ds(to * heads + c * chunk_heads, chunk_heads)]
        dst = kvbuf.at[ds(c, chunk_heads), ds(u, seq_rows), :]
        return remote(src, dst, kv_send.at[c, k], kv_recv.at[c, u], {"uly": to})

    def kv_arrival(c, k):
        s = (u + n - k) % n
        dst = kvbuf.at[ds(c, chunk_heads), ds(s, seq_rows), :]
        return remote(dst, dst, kv_send.at[c, k], kv_recv.at[c, s], {"uly": s})

    def out_copy(at, k):
        to = (u + k) % n
        src = att.at[at, ds(to, seq_rows), :]
        dst = out_ref.at[u * heads + at]
        return remote(src, dst, out_send.at[at, k], out_recv.at[at, u], {"uly": to})

    def out_arrival(at, k):
        s = (u + n - k) % n
        src = att.at[at, ds(s, seq_rows), :]
        dst = out_ref.at[s * heads + at]
        return remote(src, dst, out_send.at[at, k], out_recv.at[at, s], {"uly": s})

    def out_own(at):
        src = att.at[at, ds(u, seq_rows), :]
        return pltpu.make_async_copy(src, out_ref.at[u * heads + at], out_loc.at[at])

    for c in range(min(AHEAD, chunks)):
        own_weights(c)
    for k in range(2, n, 2):
        token_copy(k).start()
    token_mate().start()
    for k in range(1, n):
        kv_copy(0, k).start()
    for copy in own_copies:
        copy.wait()

    scale = head_width ** (-0.5)
    block = min(QUERY_ROWS, total_rows)

    def project(c):
        weight = jnp.concatenate(
            [wbuf[c * chunk_heads + h, :, :] for h in range(chunk_heads)], axis=1
        )
        if total_rows <= 512:
            qbuf[...] = jnp.dot(
                tok[...], weight, preferred_element_type=jnp.float32
            ).astype(jnp.bfloat16)
        else:
            def rows_step(r, carry):
                rows = ds(r, block)
                qbuf[rows, :] = jnp.dot(
                    tok[rows, :], weight, preferred_element_type=jnp.float32
                ).astype(jnp.bfloat16)
                return carry

            lax.fori_loop(0, total_rows // block, rows_step, 0)

    def attend(c, h):
        at = c * chunk_heads + h

        def rows_step(r, carry):
            rows = ds(r, block)
            q = qbuf[rows, h * head_width:(h + 1) * head_width]
            k = kvbuf[at, :, :head_width]
            v = kvbuf[at, :, head_width:]
            scores = lax.dot_general(
                q, k, (((1,), (1,)), ((), ())), preferred_element_type=jnp.float32
            ) * scale
            soft = jnp.exp(scores - jnp.max(scores, axis=1, keepdims=True))
            row_sum = jnp.sum(soft, axis=1, keepdims=True)
            weighted = jnp.dot(soft.astype(jnp.bfloat16), v, preferred_element_type=jnp.float32)
            att[at, rows, :] = (weighted / row_sum).astype(jnp.bfloat16)
            return carry

        lax.fori_loop(0, total_rows // block, rows_step, 0)
        for k in range(1, n):
            out_copy(at, k).start()
        out_own(at).start()

    def chunk_step(i, carry):
        c = i - LAG

        def unit(*steps):
            def run():
                @pl.when(c >= 0)
                def _():
                    for step in steps:
                        step()

            return run

        def token_pass():
            @pl.when(c == 0)
            def _():
                for k in range(2, n, 2):
                    token_arrival((u + n - k) % n).wait_recv()
                    token_forward(k).start()

        def ready():
            @pl.when(c == 0)
            def _():
                for k in range(1, n, 2):
                    token_arrival((u + n - k) % n).wait_recv()

            across_arrived(c)
            for k in range(1, n):
                kv_arrival(c, k).wait_recv()

        units = [unit(token_pass), unit(ready, lambda: project(c))]
        for h in range(chunk_heads):
            units.append(unit(functools.partial(attend, c, h)))

        @pl.when(i + AHEAD < chunks)
        def _():
            own_weights(i + AHEAD)

        pass_on(i, units)
        @pl.when(i + 1 < chunks)
        def _():
            for k in range(1, n):
                kv_copy(i + 1, k).start()

        return carry

    lax.fori_loop(0, chunks + LAG, chunk_step, 0)

    def drain(c, carry):
        weights_sent(c)
        for k in range(1, n):
            kv_copy(c, k).wait_send()
        for h in range(chunk_heads):
            at = c * chunk_heads + h
            for k in range(1, n):
                out_copy(at, k).wait_send()
                out_arrival(at, k).wait_recv()
            out_own(at).wait()
        return carry

    lax.fori_loop(0, chunks, drain, 0)
    for k in range(2, n, 2):
        token_copy(k).wait_send()
        token_forward(k).wait_send()
    token_mate().wait_send()


def body(n, blocks, tokens, query_weight, key_values):
    seq_rows, depth = tokens.shape[1:]
    shard, heads, head_width = query_weight.shape
    all_heads = key_values.shape[2]
    width = heads * head_width
    chunk_heads = CHUNK_HEADS if heads % CHUNK_HEADS == 0 else 1
    chunks = heads // chunk_heads
    cols = width // chunks
    total_rows = n * seq_rows
    dma = pltpu.SemaphoreType.DMA
    flops = 2 * total_rows * width * (depth + 2 * total_rows)
    out = pl.pallas_call(
        functools.partial(kernel, n, blocks, head_width, chunks),
        out_shape=jax.ShapeDtypeStruct((all_heads, seq_rows, head_width), jnp.bfloat16),
        in_specs=[pl.BlockSpec(memory_space=pl.ANY)] * 3,
        out_specs=pl.BlockSpec(memory_space=pl.ANY),
        scratch_shapes=[
            pltpu.VMEM((total_rows, depth), jnp.bfloat16),
            pltpu.VMEM((heads, depth, head_width), jnp.bfloat16),
            pltpu.VMEM((heads, total_rows, 2 * head_width), jnp.bfloat16),
            pltpu.VMEM((heads, total_rows, head_width), jnp.bfloat16),
            pltpu.VMEM((total_rows, cols), jnp.bfloat16),
            dma((3,)),
            dma((n,)),
            dma((n,)),
            dma((n,)),
            dma((3, chunks, blocks)),
            dma((chunks, blocks)),
            dma((2, chunks, blocks)),
            dma((chunks, blocks)),
            dma((chunks, n)),
            dma((chunks, n)),
            dma((heads, n)),
            dma((heads, n)),
            dma((heads,)),
        ],
        compiler_params=pltpu.CompilerParams(
            collective_id=0, has_side_effects=True, vmem_limit_bytes=48 * 1024 * 1024
        ),
        cost_estimate=pl.CostEstimate(
            flops=flops,
            bytes_accessed=2 * (tokens.size + query_weight.size + key_values.size),
            transcendentals=total_rows * total_rows * heads,
        ),
    )(
        tokens[0],
        jnp.transpose(query_weight, (1, 0, 2)),
        jnp.transpose(key_values[0], (1, 0, 2)),
    )
    return jnp.transpose(out, (1, 0, 2))[None]


def solution(mesh):
    return jax.shard_map(
        functools.partial(body, mesh.shape["uly"], mesh.shape["blk"]),
        mesh=mesh,
        in_specs=(P("blk", "uly", None), P("blk", "uly", None), P("blk", "uly", None, None)),
        out_specs=P("blk", "uly", None, None),
        check_vma=False,
    )
```

```python
import functools

import jax
import jax.numpy as jnp
from jax import lax
from jax.experimental import pallas as pl
from jax.experimental.pallas import tpu as pltpu
from jax.sharding import PartitionSpec as P

MESH = pl.DeviceIdType.MESH
CHUNK_HEADS = 2
AHEAD = 2
LAG = 1
QUERY_ROWS = 256


def kernel(
    n,
    blocks,
    head_width,
    chunks,
    tok_in,
    w_in,
    kv_in,
    out_ref,
    tok,
    wbuf,
    kvbuf,
    att,
    qbuf,
    kv_raw,
    kv_wide,
    kv_flat,
    loc_sem,
    tok_send,
    tok_fwd,
    tok_recv,
    w_send,
    w_recv,
    side_send,
    side_recv,
    kv_send,
    kv_recv,
    out_send,
    out_recv,
    out_loc,
):
    u = lax.axis_index("uly")
    b = lax.axis_index("blk")
    line = blocks // 2
    z = b // 2
    y = b % 2
    mate = z * 2 + (1 - y)
    core_mate = u + 1 - 2 * (u % 2)
    seq_rows = tok_in.shape[0]
    shard = w_in.shape[1]
    heads = w_in.shape[0]
    chunk_heads = heads // chunks
    side = max(16, shard // 6 // 16 * 16)
    total_rows = n * seq_rows

    def ds(start, size):
        return pl.ds(pl.multiple_of(start * size, size), size)

    def remote(src, dst, send, recv, device):
        return pltpu.make_async_remote_copy(
            src_ref=src, dst_ref=dst, send_sem=send, recv_sem=recv,
            device_id=device, device_id_type=MESH,
        )

    has_up = z < line - 1
    has_down = z > 0

    own_copies = (
        pltpu.make_async_copy(w_in, wbuf.at[:, ds(b, shard), :], loc_sem.at[0]),
        pltpu.make_async_copy(tok_in, tok.at[ds(u, seq_rows), :], loc_sem.at[1]),
        pltpu.make_async_copy(kv_in, kv_raw, loc_sem.at[2]),
    )
    for copy in own_copies:
        copy.start()

    barrier = pltpu.get_barrier_semaphore()

    def greet(device):
        pl.semaphore_signal(barrier, inc=1, device_id=device, device_id_type=MESH)

    for k in range(1, n):
        greet({"uly": (u + k) % n})
    greet({"blk": mate})

    @pl.when(has_up)
    def _():
        greet({"blk": b + 2})

    @pl.when(has_down)
    def _():
        greet({"blk": b - 2})

    inner = jnp.logical_and(has_up, has_down)

    @pl.when(inner)
    def _():
        pl.semaphore_wait(barrier, n + 2)

    @pl.when(jnp.logical_and(jnp.logical_not(inner), jnp.logical_or(has_up, has_down)))
    def _():
        pl.semaphore_wait(barrier, n + 1)

    @pl.when(jnp.logical_not(jnp.logical_or(has_up, has_down)))
    def _():
        pl.semaphore_wait(barrier, n)

    def piece(c, s):
        return wbuf.at[ds(c, chunk_heads), ds(s, shard), :]

    UP, DOWN, ACROSS = 0, 1, 2

    def w_copy(c, s, way, own=False):
        step = (2, -2, 0)[way]
        device = mate if way == ACROSS else b + step
        src = w_in.at[ds(c, chunk_heads)] if own else piece(c, s)
        return remote(src, piece(c, s), w_send.at[way, c, s], w_recv.at[c, s], {"blk": device})

    def main_copy(c, s):
        rows = pl.ds(pl.multiple_of(s * shard + side, 16), shard - side)
        part = wbuf.at[ds(c, chunk_heads), rows, :]
        return remote(part, part, w_send.at[ACROSS, c, s], w_recv.at[c, s], {"blk": mate})

    def side_copy(c, s, way):
        part = wbuf.at[
            ds(c, chunk_heads), pl.ds(pl.multiple_of(s * shard, 16), side), :
        ]
        device = b + (2, -2)[way]
        return remote(part, part, side_send.at[way, c, s], side_recv.at[c, s], {"blk": device})

    def own_weights(c):
        w_copy(c, b, ACROSS, True).start()

        @pl.when(has_up)
        def _():
            w_copy(c, b, UP, True).start()

        @pl.when(has_down)
        def _():
            w_copy(c, b, DOWN, True).start()

    def pass_on(c, between):
        ways = lambda d: (
            (UP, -2 * d, z - d >= 0, has_up),
            (DOWN, 2 * d, z + d < line, has_down),
        )

        def main(d):
            for way, step, there, more in ways(d):
                @pl.when(there)
                def _(way=way, step=step, more=more):
                    w_copy(c, b + step, ACROSS).wait_recv()

                    @pl.when(more)
                    def _():
                        w_copy(c, b + step, way).start()

                    main_copy(c, b + step).start()

        def sides(d):
            for way, step, there, more in ways(d):
                @pl.when(there)
                def _(way=way, step=step, more=more):
                    side_copy(c, mate + step, way).wait_recv()

                    @pl.when(more)
                    def _():
                        side_copy(c, mate + step, way).start()

        def forward(*steps):
            @pl.when(c < chunks)
            def _():
                for step in steps:
                    step()

        def first():
            w_copy(c, mate, ACROSS).wait_recv()

            @pl.when(has_up)
            def _():
                side_copy(c, mate, UP).start()

            @pl.when(has_down)
            def _():
                side_copy(c, mate, DOWN).start()

        forward(functools.partial(main, 1), first)
        for d in range(2, line):
            if between:
                between.pop(0)()
            forward(functools.partial(main, d), functools.partial(sides, d - 1))
        if between:
            between.pop(0)()
        forward(lambda: sides(line - 1))
        for unit in between:
            unit()

    def across_arrived(c):
        for j in range(line):
            @pl.when(j != z)
            def _():
                main_copy(c, 2 * j + 1 - y).wait_recv()

    def weights_sent(c):
        w_copy(c, b, ACROSS).wait_send()
        for j in range(line):
            s = 2 * j + y
            other = 2 * j + 1 - y

            @pl.when(j != z)
            def _():
                main_copy(c, s).wait_send()

            @pl.when(jnp.logical_and(has_up, j <= z))
            def _():
                w_copy(c, s, UP).wait_send()
                side_copy(c, other, UP).wait_send()

            @pl.when(jnp.logical_and(has_down, j >= z))
            def _():
                w_copy(c, s, DOWN).wait_send()
                side_copy(c, other, DOWN).wait_send()

    def token_rows(s):
        return tok.at[ds(s, seq_rows), :]

    def token_copy(k):
        return remote(tok_in, token_rows(u), tok_send.at[k], tok_recv.at[u], {"uly": (u + k) % n})

    def token_mate():
        return remote(tok_in, token_rows(u), tok_send.at[1], tok_recv.at[u], {"uly": core_mate})

    def token_forward(k):
        s = (u + n - k) % n
        return remote(token_rows(s), token_rows(s), tok_fwd.at[k], tok_recv.at[s], {"uly": core_mate})

    def token_arrival(s):
        return remote(token_rows(s), token_rows(s), tok_fwd.at[0], tok_recv.at[s], {"uly": core_mate})

    def kv_copy(c, k):
        to = (u + k) % n
        src = kv_flat.at[pl.ds(to * heads + c * chunk_heads, chunk_heads)]
        dst = kvbuf.at[ds(c, chunk_heads), ds(u, seq_rows), :]
        return remote(src, dst, kv_send.at[c, k], kv_recv.at[c, u], {"uly": to})

    def kv_arrival(c, k):
        s = (u + n - k) % n
        dst = kvbuf.at[ds(c, chunk_heads), ds(s, seq_rows), :]
        return remote(dst, dst, kv_send.at[c, k], kv_recv.at[c, s], {"uly": s})

    def out_copy(at, k):
        to = (u + k) % n
        src = att.at[at, ds(to, seq_rows), :]
        dst = out_ref.at[u * heads + at]
        return remote(src, dst, out_send.at[at, k], out_recv.at[at, u], {"uly": to})

    def out_arrival(at, k):
        s = (u + n - k) % n
        src = att.at[at, ds(s, seq_rows), :]
        dst = out_ref.at[s * heads + at]
        return remote(src, dst, out_send.at[at, k], out_recv.at[at, s], {"uly": s})

    def out_own(at):
        src = att.at[at, ds(u, seq_rows), :]
        return pltpu.make_async_copy(src, out_ref.at[u * heads + at], out_loc.at[at])

    for c in range(min(AHEAD, chunks)):
        own_weights(c)
    for k in range(2, n, 2):
        token_copy(k).start()
    token_mate().start()
    for copy in own_copies:
        copy.wait()

    all_heads = kv_in.shape[1]
    own_kv = pltpu.make_async_copy(
        kv_flat.at[ds(u, heads)], kvbuf.at[:, ds(u, seq_rows), :], loc_sem.at[3]
    )

    def widen():
        def rows_step(t, carry):
            part = kv_raw[ds(t, 16), :, :].astype(jnp.float32)
            for half in range(2):
                kv_wide[half, ds(t, 16 * all_heads), :] = part[
                    :, :, half * head_width:(half + 1) * head_width
                ].reshape(16 * all_heads, head_width)
            return carry

        lax.fori_loop(0, seq_rows // 16, rows_step, 0)

    def gather(start, stop):
        def head_step(h, carry):
            for half in range(2):
                rows = kv_wide[half, pl.ds(h, seq_rows, stride=all_heads), :]
                kv_flat[h, :, half * head_width:(half + 1) * head_width] = rows.astype(jnp.bfloat16)
            return carry

        lax.fori_loop(start, stop, head_step, 0)

    def send_first():
        own_kv.start()
        for k in range(1, n):
            kv_copy(0, k).start()

    scale = head_width ** (-0.5)
    block = min(QUERY_ROWS, total_rows)

    def project(c):
        weight = jnp.concatenate(
            [wbuf[c * chunk_heads + h, :, :] for h in range(chunk_heads)], axis=1
        )
        if total_rows <= 512:
            qbuf[...] = jnp.dot(
                tok[...], weight, preferred_element_type=jnp.float32
            ).astype(jnp.bfloat16)
        else:
            def rows_step(r, carry):
                rows = ds(r, block)
                qbuf[rows, :] = jnp.dot(
                    tok[rows, :], weight, preferred_element_type=jnp.float32
                ).astype(jnp.bfloat16)
                return carry

            lax.fori_loop(0, total_rows // block, rows_step, 0)

    def attend(c, h):
        at = c * chunk_heads + h

        def rows_step(r, carry):
            rows = ds(r, block)
            q = qbuf[rows, h * head_width:(h + 1) * head_width]
            k = kvbuf[at, :, :head_width]
            v = kvbuf[at, :, head_width:]
            scores = lax.dot_general(
                q, k, (((1,), (1,)), ((), ())), preferred_element_type=jnp.float32
            ) * scale
            soft = jnp.exp(scores - jnp.max(scores, axis=1, keepdims=True))
            row_sum = jnp.sum(soft, axis=1, keepdims=True)
            weighted = jnp.dot(soft.astype(jnp.bfloat16), v, preferred_element_type=jnp.float32)
            att[at, rows, :] = (weighted / row_sum).astype(jnp.bfloat16)
            return carry

        lax.fori_loop(0, total_rows // block, rows_step, 0)
        for k in range(1, n):
            out_copy(at, k).start()
        out_own(at).start()

    def chunk_step(i, carry):
        c = i - LAG

        def unit(*steps, opening=()):
            def run():
                if opening:
                    @pl.when(i == 0)
                    def _():
                        for step in opening:
                            step()

                @pl.when(c >= 0)
                def _():
                    for step in steps:
                        step()

            return run

        def token_pass():
            @pl.when(c == 0)
            def _():
                for k in range(2, n, 2):
                    token_arrival((u + n - k) % n).wait_recv()
                    token_forward(k).start()

        def ready():
            @pl.when(c == 0)
            def _():
                for k in range(1, n, 2):
                    token_arrival((u + n - k) % n).wait_recv()
                own_kv.wait()

            across_arrived(c)
            for k in range(1, n):
                kv_arrival(c, k).wait_recv()

        middle = all_heads // 2
        units = [
            unit(token_pass, opening=(widen,)),
            unit(ready, lambda: project(c), opening=(lambda: gather(0, middle),)),
            unit(
                functools.partial(attend, c, 0),
                opening=(lambda: gather(middle, all_heads), send_first),
            ),
        ]
        for h in range(1, chunk_heads):
            units.append(unit(functools.partial(attend, c, h)))

        @pl.when(i + AHEAD < chunks)
        def _():
            own_weights(i + AHEAD)

        pass_on(i, units)
        @pl.when(i + 1 < chunks)
        def _():
            for k in range(1, n):
                kv_copy(i + 1, k).start()

        return carry

    lax.fori_loop(0, chunks + LAG, chunk_step, 0)

    def drain(c, carry):
        weights_sent(c)
        for k in range(1, n):
            kv_copy(c, k).wait_send()
        for h in range(chunk_heads):
            at = c * chunk_heads + h
            for k in range(1, n):
                out_copy(at, k).wait_send()
                out_arrival(at, k).wait_recv()
            out_own(at).wait()
        return carry

    lax.fori_loop(0, chunks, drain, 0)
    for k in range(2, n, 2):
        token_copy(k).wait_send()
        token_forward(k).wait_send()
    token_mate().wait_send()


def body(n, blocks, tokens, query_weight, key_values):
    seq_rows, depth = tokens.shape[1:]
    shard, heads, head_width = query_weight.shape
    all_heads = key_values.shape[2]
    width = heads * head_width
    chunk_heads = CHUNK_HEADS if heads % CHUNK_HEADS == 0 else 1
    chunks = heads // chunk_heads
    cols = width // chunks
    total_rows = n * seq_rows
    dma = pltpu.SemaphoreType.DMA
    flops = 2 * total_rows * width * (depth + 2 * total_rows)
    out = pl.pallas_call(
        functools.partial(kernel, n, blocks, head_width, chunks),
        out_shape=jax.ShapeDtypeStruct((all_heads, seq_rows, head_width), jnp.bfloat16),
        in_specs=[pl.BlockSpec(memory_space=pl.ANY)] * 3,
        out_specs=pl.BlockSpec(memory_space=pl.ANY),
        scratch_shapes=[
            pltpu.VMEM((total_rows, depth), jnp.bfloat16),
            pltpu.VMEM((heads, depth, head_width), jnp.bfloat16),
            pltpu.VMEM((heads, total_rows, 2 * head_width), jnp.bfloat16),
            pltpu.VMEM((heads, total_rows, head_width), jnp.bfloat16),
            pltpu.VMEM((total_rows, cols), jnp.bfloat16),
            pltpu.VMEM((seq_rows, all_heads, 2 * head_width), jnp.bfloat16),
            pltpu.VMEM((2, seq_rows * all_heads, head_width), jnp.float32),
            pltpu.VMEM((all_heads, seq_rows, 2 * head_width), jnp.bfloat16),
            dma((4,)),
            dma((n,)),
            dma((n,)),
            dma((n,)),
            dma((3, chunks, blocks)),
            dma((chunks, blocks)),
            dma((2, chunks, blocks)),
            dma((chunks, blocks)),
            dma((chunks, n)),
            dma((chunks, n)),
            dma((heads, n)),
            dma((heads, n)),
            dma((heads,)),
        ],
        compiler_params=pltpu.CompilerParams(
            collective_id=0, has_side_effects=True, vmem_limit_bytes=60 * 1024 * 1024
        ),
        cost_estimate=pl.CostEstimate(
            flops=flops,
            bytes_accessed=2 * (tokens.size + query_weight.size + key_values.size),
            transcendentals=total_rows * total_rows * heads,
        ),
    )(
        tokens[0],
        jnp.transpose(query_weight, (1, 0, 2)),
        key_values[0],
    )
    return jnp.transpose(out, (1, 0, 2))[None]


def solution(mesh):
    return jax.shard_map(
        functools.partial(body, mesh.shape["uly"], mesh.shape["blk"]),
        mesh=mesh,
        in_specs=(P("blk", "uly", None), P("blk", "uly", None), P("blk", "uly", None, None)),
        out_specs=P("blk", "uly", None, None),
        check_vma=False,
    )
```

```python
import functools

import jax
import jax.numpy as jnp
from jax import lax
from jax.experimental import pallas as pl
from jax.experimental.pallas import tpu as pltpu
from jax.sharding import PartitionSpec as P

MESH = pl.DeviceIdType.MESH
CHUNK_HEADS = 2
AHEAD = 2
LAG = 1
QUERY_ROWS = 256


def kernel(
    n,
    blocks,
    head_width,
    chunks,
    tok_in,
    w_in,
    kv_in,
    out_ref,
    tok,
    wbuf,
    kvbuf,
    att,
    qbuf,
    kv_raw,
    kv_wide,
    kv_flat,
    loc_sem,
    tok_send,
    tok_fwd,
    tok_recv,
    w_send,
    w_recv,
    side_send,
    side_recv,
    kv_send,
    kv_recv,
    out_send,
    out_recv,
    out_loc,
):
    u = lax.axis_index("uly")
    b = lax.axis_index("blk")
    line = blocks // 2
    z = b // 2
    y = b % 2
    mate = z * 2 + (1 - y)
    core_mate = u + 1 - 2 * (u % 2)
    seq_rows = tok_in.shape[0]
    shard = w_in.shape[1]
    heads = w_in.shape[0]
    chunk_heads = heads // chunks
    side = max(16, shard // 6 // 16 * 16)
    total_rows = n * seq_rows

    def ds(start, size):
        return pl.ds(pl.multiple_of(start * size, size), size)

    def remote(src, dst, send, recv, device):
        return pltpu.make_async_remote_copy(
            src_ref=src, dst_ref=dst, send_sem=send, recv_sem=recv,
            device_id=device, device_id_type=MESH,
        )

    has_up = z < line - 1
    has_down = z > 0

    own_copies = (
        pltpu.make_async_copy(w_in, wbuf.at[:, ds(b, shard), :], loc_sem.at[0]),
        pltpu.make_async_copy(tok_in, tok.at[ds(u, seq_rows), :], loc_sem.at[1]),
        pltpu.make_async_copy(kv_in, kv_raw, loc_sem.at[2]),
    )
    for copy in own_copies:
        copy.start()

    barrier = pltpu.get_barrier_semaphore()

    def greet(device):
        pl.semaphore_signal(barrier, inc=1, device_id=device, device_id_type=MESH)

    for k in range(1, n):
        greet({"uly": (u + k) % n})
    greet({"blk": mate})

    @pl.when(has_up)
    def _():
        greet({"blk": b + 2})

    @pl.when(has_down)
    def _():
        greet({"blk": b - 2})

    inner = jnp.logical_and(has_up, has_down)

    @pl.when(inner)
    def _():
        pl.semaphore_wait(barrier, n + 2)

    @pl.when(jnp.logical_and(jnp.logical_not(inner), jnp.logical_or(has_up, has_down)))
    def _():
        pl.semaphore_wait(barrier, n + 1)

    @pl.when(jnp.logical_not(jnp.logical_or(has_up, has_down)))
    def _():
        pl.semaphore_wait(barrier, n)

    def piece(c, s):
        return wbuf.at[ds(c, chunk_heads), ds(s, shard), :]

    UP, DOWN, ACROSS = 0, 1, 2

    def w_copy(c, s, way, own=False):
        step = (2, -2, 0)[way]
        device = mate if way == ACROSS else b + step
        src = w_in.at[ds(c, chunk_heads)] if own else piece(c, s)
        return remote(src, piece(c, s), w_send.at[way, c, s], w_recv.at[c, s], {"blk": device})

    def main_copy(c, s):
        rows = pl.ds(pl.multiple_of(s * shard + side, 16), shard - side)
        part = wbuf.at[ds(c, chunk_heads), rows, :]
        return remote(part, part, w_send.at[ACROSS, c, s], w_recv.at[c, s], {"blk": mate})

    def side_copy(c, s, way):
        part = wbuf.at[
            ds(c, chunk_heads), pl.ds(pl.multiple_of(s * shard, 16), side), :
        ]
        device = b + (2, -2)[way]
        return remote(part, part, side_send.at[way, c, s], side_recv.at[c, s], {"blk": device})

    def own_weights(c):
        w_copy(c, b, ACROSS, True).start()

        @pl.when(has_up)
        def _():
            w_copy(c, b, UP, True).start()

        @pl.when(has_down)
        def _():
            w_copy(c, b, DOWN, True).start()

    def pass_on(c, between):
        ways = lambda d: (
            (UP, -2 * d, z - d >= 0, has_up),
            (DOWN, 2 * d, z + d < line, has_down),
        )

        def main(d):
            for way, step, there, more in ways(d):
                @pl.when(there)
                def _(way=way, step=step, more=more):
                    w_copy(c, b + step, ACROSS).wait_recv()

                    @pl.when(more)
                    def _():
                        w_copy(c, b + step, way).start()

                    main_copy(c, b + step).start()

        def sides(d):
            for way, step, there, more in ways(d):
                @pl.when(there)
                def _(way=way, step=step, more=more):
                    side_copy(c, mate + step, way).wait_recv()

                    @pl.when(more)
                    def _():
                        side_copy(c, mate + step, way).start()

        def forward(*steps):
            @pl.when(c < chunks)
            def _():
                for step in steps:
                    step()

        def first():
            w_copy(c, mate, ACROSS).wait_recv()

            @pl.when(has_up)
            def _():
                side_copy(c, mate, UP).start()

            @pl.when(has_down)
            def _():
                side_copy(c, mate, DOWN).start()

        forward(functools.partial(main, 1), first)
        for d in range(2, line):
            if between:
                between.pop(0)()
            forward(functools.partial(main, d), functools.partial(sides, d - 1))
        if between:
            between.pop(0)()
        forward(lambda: sides(line - 1))
        for unit in between:
            unit()

    def across_arrived(c):
        for j in range(line):
            @pl.when(j != z)
            def _():
                main_copy(c, 2 * j + 1 - y).wait_recv()

    def weights_sent(c):
        w_copy(c, b, ACROSS).wait_send()
        for j in range(line):
            s = 2 * j + y
            other = 2 * j + 1 - y

            @pl.when(j != z)
            def _():
                main_copy(c, s).wait_send()

            @pl.when(jnp.logical_and(has_up, j <= z))
            def _():
                w_copy(c, s, UP).wait_send()
                side_copy(c, other, UP).wait_send()

            @pl.when(jnp.logical_and(has_down, j >= z))
            def _():
                w_copy(c, s, DOWN).wait_send()
                side_copy(c, other, DOWN).wait_send()

    def token_rows(s):
        return tok.at[ds(s, seq_rows), :]

    def token_copy(k):
        return remote(tok_in, token_rows(u), tok_send.at[k], tok_recv.at[u], {"uly": (u + k) % n})

    def token_mate():
        return remote(tok_in, token_rows(u), tok_send.at[1], tok_recv.at[u], {"uly": core_mate})

    def token_forward(k):
        s = (u + n - k) % n
        return remote(token_rows(s), token_rows(s), tok_fwd.at[k], tok_recv.at[s], {"uly": core_mate})

    def token_arrival(s):
        return remote(token_rows(s), token_rows(s), tok_fwd.at[0], tok_recv.at[s], {"uly": core_mate})

    def kv_copy(c, k):
        to = (u + k) % n
        src = kv_flat.at[pl.ds(to * heads + c * chunk_heads, chunk_heads)]
        dst = kvbuf.at[ds(c, chunk_heads), ds(u, seq_rows), :]
        return remote(src, dst, kv_send.at[c, k], kv_recv.at[c, u], {"uly": to})

    def kv_arrival(c, k):
        s = (u + n - k) % n
        dst = kvbuf.at[ds(c, chunk_heads), ds(s, seq_rows), :]
        return remote(dst, dst, kv_send.at[c, k], kv_recv.at[c, s], {"uly": s})

    def out_copy(at, k):
        to = (u + k) % n
        src = att.at[at, ds(to, seq_rows), :]
        dst = out_ref.at[u * heads + at]
        return remote(src, dst, out_send.at[at, k], out_recv.at[at, u], {"uly": to})

    def out_arrival(at, k):
        s = (u + n - k) % n
        src = att.at[at, ds(s, seq_rows), :]
        dst = out_ref.at[s * heads + at]
        return remote(src, dst, out_send.at[at, k], out_recv.at[at, s], {"uly": s})

    def out_own(at):
        src = att.at[at, ds(u, seq_rows), :]
        return pltpu.make_async_copy(src, out_ref.at[u * heads + at], out_loc.at[at])

    for c in range(min(AHEAD, chunks)):
        own_weights(c)
    for k in range(2, n, 2):
        token_copy(k).start()
    token_mate().start()
    for copy in own_copies:
        copy.wait()

    all_heads = kv_in.shape[1]
    own_kv = pltpu.make_async_copy(
        kv_flat.at[ds(u, heads)], kvbuf.at[:, ds(u, seq_rows), :], loc_sem.at[3]
    )

    def widen():
        def rows_step(t, carry):
            part = kv_raw[ds(t, 16), :, :].astype(jnp.float32)
            for half in range(2):
                kv_wide[half, ds(t, 16 * all_heads), :] = part[
                    :, :, half * head_width:(half + 1) * head_width
                ].reshape(16 * all_heads, head_width)
            return carry

        lax.fori_loop(0, seq_rows // 16, rows_step, 0)

    def gather(start, stop):
        def head_step(h, carry):
            for half in range(2):
                rows = kv_wide[half, pl.ds(h, seq_rows, stride=all_heads), :]
                kv_flat[h, :, half * head_width:(half + 1) * head_width] = rows.astype(jnp.bfloat16)
            return carry

        lax.fori_loop(start, stop, head_step, 0)

    def send_first():
        own_kv.start()
        for k in range(1, n):
            kv_copy(0, k).start()

    scale = head_width ** (-0.5)
    block = min(QUERY_ROWS, total_rows)

    def project(c):
        weight = jnp.concatenate(
            [wbuf[c * chunk_heads + h, :, :] for h in range(chunk_heads)], axis=1
        )
        if total_rows <= 512:
            qbuf[...] = jnp.dot(
                tok[...], weight, preferred_element_type=jnp.float32
            ).astype(jnp.bfloat16)
        else:
            def rows_step(r, carry):
                rows = ds(r, block)
                qbuf[rows, :] = jnp.dot(
                    tok[rows, :], weight, preferred_element_type=jnp.float32
                ).astype(jnp.bfloat16)
                return carry

            lax.fori_loop(0, total_rows // block, rows_step, 0)

    def attend(c, h):
        at = c * chunk_heads + h

        def rows_step(r, carry):
            rows = ds(r, block)
            q = qbuf[rows, h * head_width:(h + 1) * head_width]
            k = kvbuf[at, :, :head_width]
            v = kvbuf[at, :, head_width:]
            scores = lax.dot_general(
                q, k, (((1,), (1,)), ((), ())), preferred_element_type=jnp.float32
            ) * scale
            soft = jnp.exp(scores - jnp.max(scores, axis=1, keepdims=True))
            row_sum = jnp.sum(soft, axis=1, keepdims=True)
            weighted = jnp.dot(soft.astype(jnp.bfloat16), v, preferred_element_type=jnp.float32)
            att[at, rows, :] = (weighted / row_sum).astype(jnp.bfloat16)
            return carry

        lax.fori_loop(0, total_rows // block, rows_step, 0)
        for k in range(1, n):
            out_copy(at, k).start()
        out_own(at).start()

    def chunk_step(i, carry):
        c = i - LAG

        def unit(*steps, opening=()):
            def run():
                if opening:
                    @pl.when(i == 0)
                    def _():
                        for step in opening:
                            step()

                @pl.when(c >= 0)
                def _():
                    for step in steps:
                        step()

            return run

        def token_pass():
            @pl.when(c == 0)
            def _():
                for k in range(2, n, 2):
                    token_arrival((u + n - k) % n).wait_recv()
                    token_forward(k).start()

        def ready():
            @pl.when(c == 0)
            def _():
                for k in range(1, n, 2):
                    token_arrival((u + n - k) % n).wait_recv()
                own_kv.wait()

            across_arrived(c)
            for k in range(1, n):
                kv_arrival(c, k).wait_recv()

        middle = all_heads // 2
        units = [
            unit(token_pass, opening=(widen,)),
            unit(ready, lambda: project(c), opening=(lambda: gather(0, middle),)),
            unit(
                functools.partial(attend, c, 0),
                opening=(lambda: gather(middle, all_heads), send_first),
            ),
        ]
        for h in range(1, chunk_heads):
            units.append(unit(functools.partial(attend, c, h)))

        @pl.when(i + AHEAD < chunks)
        def _():
            own_weights(i + AHEAD)

        pass_on(i, units)
        @pl.when(i + 1 < chunks)
        def _():
            for k in range(1, n):
                kv_copy(i + 1, k).start()

        return carry

    lax.fori_loop(0, chunks + LAG, chunk_step, 0)

    def drain(c, carry):
        weights_sent(c)
        for k in range(1, n):
            kv_copy(c, k).wait_send()
        for h in range(chunk_heads):
            at = c * chunk_heads + h
            for k in range(1, n):
                out_copy(at, k).wait_send()
                out_arrival(at, k).wait_recv()
            out_own(at).wait()
        return carry

    lax.fori_loop(0, chunks, drain, 0)
    for k in range(2, n, 2):
        token_copy(k).wait_send()
        token_forward(k).wait_send()
    token_mate().wait_send()


def body(n, blocks, tokens, query_weight, key_values):
    seq_rows, depth = tokens.shape[1:]
    shard, heads, head_width = query_weight.shape
    all_heads = key_values.shape[2]
    width = heads * head_width
    chunk_heads = CHUNK_HEADS if heads % CHUNK_HEADS == 0 else 1
    chunks = heads // chunk_heads
    cols = width // chunks
    total_rows = n * seq_rows
    dma = pltpu.SemaphoreType.DMA
    flops = 2 * total_rows * width * (depth + 2 * total_rows)
    out = pl.pallas_call(
        functools.partial(kernel, n, blocks, head_width, chunks),
        out_shape=jax.ShapeDtypeStruct((all_heads, seq_rows, head_width), jnp.bfloat16),
        in_specs=[pl.BlockSpec(memory_space=pl.ANY)] * 3,
        out_specs=pl.BlockSpec(memory_space=pl.ANY),
        scratch_shapes=[
            pltpu.VMEM((total_rows, depth), jnp.bfloat16),
            pltpu.VMEM((heads, depth, head_width), jnp.bfloat16),
            pltpu.VMEM((heads, total_rows, 2 * head_width), jnp.bfloat16),
            pltpu.VMEM((heads, total_rows, head_width), jnp.bfloat16),
            pltpu.VMEM((total_rows, cols), jnp.bfloat16),
            pltpu.VMEM((seq_rows, all_heads, 2 * head_width), jnp.bfloat16),
            pltpu.VMEM((2, seq_rows * all_heads, head_width), jnp.float32),
            pltpu.VMEM((all_heads, seq_rows, 2 * head_width), jnp.bfloat16),
            dma((4,)),
            dma((n,)),
            dma((n,)),
            dma((n,)),
            dma((3, chunks, blocks)),
            dma((chunks, blocks)),
            dma((2, chunks, blocks)),
            dma((chunks, blocks)),
            dma((chunks, n)),
            dma((chunks, n)),
            dma((heads, n)),
            dma((heads, n)),
            dma((heads,)),
        ],
        compiler_params=pltpu.CompilerParams(
            collective_id=0, has_side_effects=True, vmem_limit_bytes=51 * 1024 * 1024
        ),
        cost_estimate=pl.CostEstimate(
            flops=flops,
            bytes_accessed=2 * (tokens.size + query_weight.size + key_values.size),
            transcendentals=total_rows * total_rows * heads,
        ),
    )(
        tokens[0],
        jnp.transpose(query_weight, (1, 0, 2)),
        key_values[0],
    )
    return jnp.transpose(out, (1, 0, 2))[None]


def solution(mesh):
    return jax.shard_map(
        functools.partial(body, mesh.shape["uly"], mesh.shape["blk"]),
        mesh=mesh,
        in_specs=(P("blk", "uly", None), P("blk", "uly", None), P("blk", "uly", None, None)),
        out_specs=P("blk", "uly", None, None),
        check_vma=False,
    )
```
